128 devices in a mesh: gx: 64 (over y, x, z_lo, core), gy: 2 (over z_hi).
Axes of the slice: x: 4, y: 4, z: 4 (z_hi: 2, z_lo: 2; z = z_hi * 2 + z_lo), core: 2. Of those that a mesh axis runs over, the one named last changes fastest.
Arguments:
- field: float32 [2, 2048, 256, 128], P(None, 'gx', 'gy'), may hold values from -6 to 6
- source: float32 [2, 2048, 256, 128], P(None, 'gx', 'gy'), may hold values from -6 to 6
- wavenum_sq: float32 [2048, 256, 128], P('gx', 'gy'), may hold values from 2.47 to 4.8
- coupling_x: float32 [8, 8], replicated, may hold values from -2 to 2
- coupling_y: float32 [8, 8], replicated, may hold values from -2 to 2
Outputs:
- updated: float32 [2, 2048, 256, 128], P(None, 'gx', 'gy')
The draws below stay inside these ranges and needn't reach their ends.
All inputs are finite; a program needn't handle non-finite values.
Results may differ from the reference program's by a relative error of at most 0.0001.
Values sent between devices are 32-bit elements; how exact they have to be, the bound alone decides.
No kernel may reach another device: no remote copies, remote signals or barrier semaphores. Data moves between devices by JAX's collectives and lax.ppermute only.
A program may use at most 128 MiB of HBM per device.

```python
import jax
import jax.numpy as jnp
from jax import lax

CX = 32
CY = 128
NZ = 128
RIM = 8
ITERS = 2
NX = 2048
NY = 256
N_GX = 64
N_GY = 2


def shard_levels(stream_key, shape, split, least, top_value):
    def one(position, blocks):
        draws = jax.random.uniform(jax.random.fold_in(jax.random.fold_in(stream_key, 6), position), (blocks,), jnp.float32, least / len(split), top_value / len(split))
        return jnp.repeat(jnp.exp(draws), shape[position] // blocks).reshape((-1,) + (1,) * (len(shape) - position - 1))

    level = one(*split[0])
    for cut in split[1:]:
        level = level * one(*cut)
    return level


def scatter_about(stream_key, dims, width, bound, split=(), dtype=jnp.bfloat16):
    array = jax.random.normal(stream_key, dims, jnp.float32) * width
    if len(split) > 0:
        array = shard_levels(stream_key, dims, split, -0.22, 0.18) * array
    return jnp.clip(array, min=-bound, max=bound).astype(dtype)


def setup_inputs(seed: int = 0) -> dict:
    arg_keys = jax.random.split(jax.random.key(seed), 6)
    return {
        "field": scatter_about(arg_keys[0], (2, NX, NY, NZ), 1.0, 6.0, ((1, 64), (2, 2)), jnp.float32),
        "source": scatter_about(arg_keys[1], (2, NX, NY, NZ), 1.0, 6.0, ((1, 64), (2, 2)), jnp.float32),
        "wavenum_sq": jnp.clip(2.47 + 2.3300002 * jax.random.uniform(arg_keys[2], (NX, NY, NZ), jnp.float32) ** shard_levels(arg_keys[2], (NX, NY, NZ), ((0, 64), (1, 2)), -0.2, 0.2), 2.47, 4.8),
        "coupling_x": scatter_about(arg_keys[3], (RIM, RIM), RIM ** -0.5, 2.0, (), jnp.float32),
        "coupling_y": scatter_about(arg_keys[4], (RIM, RIM), RIM ** -0.5, 2.0, (), jnp.float32),
    }


K0SQ = 2.4674
EPS = 2.5


def signed_sq(length):
    freq = 2.0 * jnp.pi * jnp.fft.fftfreq(length)
    return freq * freq


def correction(wave, coupling_x, coupling_y):
    high = lax.Precision.HIGHEST
    blocks = wave.reshape(2, N_GX, CX, NY, NZ)
    own_lo = blocks[:, :, :RIM]
    own_hi = blocks[:, :, CX - RIM:][:, :, ::-1]
    prev_hi = jnp.concatenate([jnp.zeros_like(own_hi[:, :1]), own_hi[:, :-1]], axis=1)
    next_lo = jnp.concatenate([own_lo[:, 1:], jnp.zeros_like(own_lo[:, :1])], axis=1)
    low_term = jnp.einsum("ab,pgbyz->pgayz", coupling_x, prev_hi - own_hi, precision=high)
    high_term = jnp.einsum("ab,pgbyz->pgayz", coupling_x, next_lo - own_lo, precision=high)[:, :, ::-1]
    middle = jnp.zeros((2, N_GX, CX - 2 * RIM, NY, NZ), jnp.float32)
    along_x = jnp.concatenate([low_term, middle, high_term], axis=2).reshape(2, NX, NY, NZ)
    blocks = wave.reshape(2, NX, N_GY, CY, NZ)
    own_lo = blocks[:, :, :, :RIM]
    own_hi = blocks[:, :, :, CY - RIM:][:, :, :, ::-1]
    prev_hi = jnp.concatenate([jnp.zeros_like(own_hi[:, :, :1]), own_hi[:, :, :-1]], axis=2)
    next_lo = jnp.concatenate([own_lo[:, :, 1:], jnp.zeros_like(own_lo[:, :, :1])], axis=2)
    low_term = jnp.einsum("ab,pxgbz->pxgaz", coupling_y, prev_hi - own_hi, precision=high)
    high_term = jnp.einsum("ab,pxgbz->pxgaz", coupling_y, next_lo - own_lo, precision=high)[:, :, :, ::-1]
    middle = jnp.zeros((2, NX, N_GY, CY - 2 * RIM, NZ), jnp.float32)
    along_y = jnp.concatenate([low_term, middle, high_term], axis=3).reshape(2, NX, NY, NZ)
    return along_x + along_y


def block_green(wave):
    psq = signed_sq(CX)[:, None, None] + signed_sq(CY)[None, :, None] + signed_sq(NZ)[None, None, :]
    offset = psq - K0SQ
    denom = offset * offset + EPS * EPS
    green = offset / denom + 1j * (EPS / denom)
    cplx = (wave[0] + 1j * wave[1]).reshape(N_GX, CX, N_GY, CY, NZ)

    def per_slab(slab):
        spectrum = jnp.fft.fftn(slab, axes=(0, 2, 3))
        return jnp.fft.ifftn(spectrum * green[:, None], axes=(0, 2, 3))

    result = lax.map(per_slab, cplx).reshape(NX, NY, NZ)
    return jnp.stack([jnp.real(result), jnp.imag(result)]).astype(jnp.float32)


def reference(field, source, wavenum_sq, coupling_x, coupling_y):
    shifted = wavenum_sq - K0SQ
    wave = field
    for step in range(ITERS):
        fixes = correction(wave, coupling_x, coupling_y)
        pot_re = shifted * wave[0] + EPS * wave[1]
        pot_im = shifted * wave[1] - EPS * wave[0]
        mixed = jnp.stack([pot_re, pot_im]) - fixes + source
        greened = block_green(mixed)
        resid = wave - greened
        ratio = shifted / EPS
        damped = jnp.stack([resid[0] - ratio * resid[1], resid[1] + ratio * resid[0]])
        wave = wave - damped
    return wave
```

```python
import functools
import math

import jax
import jax.numpy as jnp
import ml_dtypes
import numpy as np
from jax import lax
from jax.experimental import pallas as pl
from jax.experimental.pallas import tpu as pltpu
from jax.sharding import PartitionSpec as P

RIM = 8
K0SQ = 2.4674
EPS = 2.5
CX = 32
N = 128
BF = jnp.bfloat16
F32 = jnp.float32
VMEM_LIMIT = 40 * 1024 * 1024


def two_halves(table):
    high = table.astype(ml_dtypes.bfloat16)
    low = (table - high.astype(np.float64)).astype(ml_dtypes.bfloat16)
    return np.stack([high, low])


def dft_tables():
    index = np.arange(N)
    angle = 2.0 * np.pi / N * (index[:, None] * index[None, :] % N)
    cosine, sine = np.cos(angle), np.sin(angle)
    z_forward = np.block([[cosine, -sine], [sine, cosine]])
    z_inverse = np.block([[cosine, sine], [-sine, cosine]])
    return (
        two_halves(z_forward),
        two_halves(z_inverse),
        two_halves(z_forward.T),
        two_halves(z_inverse.T),
    )


def angular_sq(length):
    freq = 2.0 * np.pi * np.fft.fftfreq(length)
    return freq * freq


def green_table():
    psq = (
        angular_sq(CX)[: CX // 2 + 1, None, None]
        + angular_sq(N)[None, :, None]
        + angular_sq(N)[None, None, :]
    )
    offset = psq - K0SQ
    denom = (offset * offset + EPS * EPS) * (CX * N * N)
    return np.stack([offset / denom, EPS / denom], axis=1).astype(np.float32)


def halves(value):
    high = value.astype(BF)
    return high, (value - high.astype(F32)).astype(BF)


def from_right(value, table):
    high, low = halves(value)
    out = jnp.dot(high, table[0], preferred_element_type=F32)
    out += jnp.dot(low, table[0], preferred_element_type=F32)
    return out + jnp.dot(high, table[1], preferred_element_type=F32)


def from_left(table, value):
    high, low = halves(value)
    out = jnp.dot(table[0], high, preferred_element_type=F32)
    out += jnp.dot(table[0], low, preferred_element_type=F32)
    return out + jnp.dot(table[1], high, preferred_element_type=F32)


def by_rows(re0, im0, re1, im1):
    return jnp.concatenate(
        [jnp.concatenate([re0, im0], axis=1), jnp.concatenate([re1, im1], axis=1)], axis=0
    )


def swap_blocks(value):
    return jnp.concatenate(
        [
            jnp.concatenate([value[:N, :N], value[N:, :N]], axis=1),
            jnp.concatenate([value[:N, N:], value[N:, N:]], axis=1),
        ],
        axis=0,
    )


def times_root(value, step, length):
    re, im = value
    step %= length
    if step == 0:
        return value
    if 4 * step == length:
        return -im, re
    if 2 * step == length:
        return -re, -im
    if 4 * step == 3 * length:
        return im, -re
    c = math.cos(2.0 * math.pi * step / length)
    s = math.sin(2.0 * math.pi * step / length)
    if 8 * step % length == 0:
        h = math.sqrt(0.5)
        sc, ss = math.copysign(1.0, c), math.copysign(1.0, s)
        first = re - im if sc == ss else re + im
        second = re + im if sc == ss else im - re
        return first * (h * sc), second * (h * sc)
    return re * c - im * s, re * s + im * c


def fft(values, sign):
    count = len(values)
    if count == 1:
        return values
    even = fft(values[0::2], sign)
    odd = fft(values[1::2], sign)
    first, second = [], []
    for k in range(count // 2):
        re, im = times_root(odd[k], sign * k, count)
        first.append((even[k][0] + re, even[k][1] + im))
        second.append((even[k][0] - re, even[k][1] - im))
    return first + second


def filter_x(load, store, green, rows):
    spectrum = fft([load(x) for x in range(CX)], -1)
    scaled = []
    for k, (re, im) in enumerate(spectrum):
        g_re = green[min(k, CX - k), 0, rows, :]
        g_im = green[min(k, CX - k), 1, rows, :]
        scaled.append((re * g_re - im * g_im, re * g_im + im * g_re))
    for x, value in enumerate(fft(scaled, 1)):
        store(x, value)


def local_kernel(
    side_ref, mix_x_ref, mix_y_ref, field_ref, source_ref, wave_ref, low_ref, high_ref, near_ref,
    z_ref, y_ref, out_ref, work_ref,
):
    block = pl.program_id(0)
    planes = field_ref.shape[1]
    for p in range(planes):
        shifted = wave_ref[p] - K0SQ
        re, im = field_ref[0, p], field_ref[1, p]
        work_ref[0, p] = shifted * re + EPS * im + source_ref[0, p]
        work_ref[1, p] = shifted * im - EPS * re + source_ref[1, p]
        for part in range(2):
            first = field_ref[part, p, 0:RIM, :]
            last = field_ref[part, p, N - RIM : N, :]
            add_low = mix_y_ref[0, 0] * last[0:1]
            add_high = mix_y_ref[1, 0] * first[0:1]
            for b in range(1, RIM):
                add_low += mix_y_ref[0, b] * last[b : b + 1]
                add_high += mix_y_ref[1, b] * first[b : b + 1]
            work_ref[part, p, 0:RIM, :] += add_low
            work_ref[part, p, N - RIM : N, :] += add_high

    def along_x(base, other_ref, weight):
        @pl.loop(0, N // 16)
        def _(t):
            rows = pl.ds(pl.multiple_of(t * 16, 16), 16)
            for part in range(2):
                source = [
                    other_ref[part, r, rows, :] - weight * near_ref[part, r, rows, :]
                    for r in range(RIM)
                ]
                for p in range(planes):
                    total = work_ref[part, p, rows, :]
                    for r in range(RIM):
                        total += mix_x_ref[base + p, r] * source[r]
                    work_ref[part, p, rows, :] = total

    low_blocks = RIM // planes

    @pl.when(block < low_blocks)
    def _():
        along_x(block * planes, high_ref, side_ref[0])

    @pl.when(block >= (CX - RIM) // planes)
    def _():
        along_x(RIM + block * planes - (CX - RIM), low_ref, side_ref[1])

    for p in range(0, planes, 2):
        wide = from_right(
            by_rows(work_ref[0, p], work_ref[1, p], work_ref[0, p + 1], work_ref[1, p + 1]), z_ref
        )
        tall = from_left(y_ref, swap_blocks(wide))
        out_ref[0, p] = tall[:N, :N]
        out_ref[1, p] = tall[N:, :N]
        out_ref[0, p + 1] = tall[:N, N:]
        out_ref[1, p + 1] = tall[N:, N:]


def side_kernel(mix_ref, face_ref, hat_ref, z_ref, table_ref, out_ref, rows_ref, wide_ref):
    @pl.loop(0, CX)
    def _(x):
        for part in range(2):
            tile = face_ref[part, x]
            total = mix_ref[0] * tile[0:1]
            for b in range(1, RIM):
                total += mix_ref[b] * tile[b : b + 1]
            rows_ref[pl.ds(pl.multiple_of(x * RIM, RIM), RIM), part * N : (part + 1) * N] = -total

    wide_ref[...] = from_right(rows_ref[...], z_ref)

    @pl.loop(0, CX // 2)
    def _(pair):
        rows = wide_ref[pl.ds(pl.multiple_of(pair * 2 * RIM, 2 * RIM), 2 * RIM), :]
        short = jnp.concatenate(
            [
                jnp.concatenate([rows[:RIM, :N], rows[RIM:, :N]], axis=1),
                jnp.concatenate([rows[:RIM, N:], rows[RIM:, N:]], axis=1),
            ],
            axis=0,
        )
        tall = from_left(table_ref, short)
        x = pair * 2
        out_ref[0, x] = hat_ref[0, x] + tall[:N, :N]
        out_ref[1, x] = hat_ref[1, x] + tall[N:, :N]
        out_ref[0, x + 1] = hat_ref[0, x + 1] + tall[:N, N:]
        out_ref[1, x + 1] = hat_ref[1, x + 1] + tall[N:, N:]


def far_kernel(
    side_ref, mix_ref, face_ref, hat_ref, z_ref, y_ref, green_ref, out_ref, work_ref
):
    @pl.loop(0, N // 16)
    def _(t):
        rows = pl.ds(pl.multiple_of(t * 16, 16), 16)
        for part in range(2):
            source = [face_ref[part, r, rows, :] for r in range(RIM)]
            for p in range(RIM):
                total = mix_ref[p, 0] * source[0]
                for r in range(1, RIM):
                    total += mix_ref[p, r] * source[r]
                work_ref[part, p, rows, :] = -total

    @pl.loop(0, RIM // 2)
    def _(pair):
        p = pair * 2
        wide = from_right(
            by_rows(work_ref[0, p], work_ref[1, p], work_ref[0, p + 1], work_ref[1, p + 1]), z_ref
        )
        tall = from_left(y_ref, swap_blocks(wide))
        work_ref[0, p] = tall[:N, :N]
        work_ref[1, p] = tall[N:, :N]
        work_ref[0, p + 1] = tall[:N, N:]
        work_ref[1, p + 1] = tall[N:, N:]

    @pl.loop(0, N // 8)
    def _(t):
        rows = pl.ds(pl.multiple_of(t * 8, 8), 8)

        def load(x):
            re, im = hat_ref[0, x, rows, :], hat_ref[1, x, rows, :]
            if x < RIM or x >= CX - RIM:
                weight = side_ref[int(x < RIM)]
                re += weight * work_ref[0, x % RIM, rows, :]
                im += weight * work_ref[1, x % RIM, rows, :]
            return re, im

        def store(x, value):
            out_ref[0, x, rows, :] = value[0]
            out_ref[1, x, rows, :] = value[1]

        filter_x(load, store, green_ref, rows)


def back_kernel(hat_ref, field_ref, wave_ref, y_ref, z_ref, out_ref):
    for p in range(0, field_ref.shape[1], 2):
        tall = jnp.concatenate(
            [
                jnp.concatenate([hat_ref[0, p], hat_ref[0, p + 1]], axis=1),
                jnp.concatenate([hat_ref[1, p], hat_ref[1, p + 1]], axis=1),
            ],
            axis=0,
        )
        wide = from_right(swap_blocks(from_left(y_ref, tall)), z_ref)
        for q in range(2):
            ratio = (wave_ref[p + q] - K0SQ) * (1.0 / EPS)
            re, im = field_ref[0, p + q], field_ref[1, p + q]
            r_re = re - wide[q * N : (q + 1) * N, :N]
            r_im = im - wide[q * N : (q + 1) * N, N:]
            out_ref[0, p + q] = re - (r_re - ratio * r_im)
            out_ref[1, p + q] = im - (r_im + ratio * r_re)


SMEM = pl.BlockSpec(memory_space=pltpu.SMEM)
WHOLE = pl.BlockSpec(memory_space=pltpu.VMEM)
VOLUME = jax.ShapeDtypeStruct((2, CX, N, N), F32)
PARAMS = pltpu.CompilerParams(vmem_limit_bytes=VMEM_LIMIT)


def cost(flops, size):
    return pl.CostEstimate(flops=flops, bytes_accessed=size, transcendentals=0)


def whole(shape):
    return pl.BlockSpec(shape, lambda i: (0,) * len(shape))


def local(side, mix_x, mix_y, field, source, wave, near, z_table, y_table):
    planes = 4
    volume = pl.BlockSpec((2, planes, N, N), lambda i: (0, i, 0, 0))
    return pl.pallas_call(
        local_kernel,
        grid=(CX // planes,),
        in_specs=[
            SMEM, SMEM, whole((2, RIM, RIM, N)), volume, volume,
            pl.BlockSpec((planes, N, N), lambda i: (i, 0, 0)),
            pl.BlockSpec((2, RIM, N, N), lambda i: (0, 0, 0, 0)),
            pl.BlockSpec((2, RIM, N, N), lambda i: (0, CX // RIM - 1, 0, 0)),
            whole((2, RIM, N, N)), whole((2, 256, 256)), whole((2, 256, 256)),
        ],
        out_specs=volume,
        out_shape=VOLUME,
        scratch_shapes=[pltpu.VMEM((2, planes, N, N), F32)],
        compiler_params=PARAMS,
        cost_estimate=cost(8 * 10**9, 14 * 2**20),
    )(side, mix_x, mix_y, field, source, wave, field, field, near, z_table, y_table)


def add_side(mix, face, hat, z_table, table):
    return pl.pallas_call(
        side_kernel,
        in_specs=[WHOLE] * 5,
        out_specs=WHOLE,
        out_shape=VOLUME,
        scratch_shapes=[pltpu.VMEM((CX * RIM, 256), F32), pltpu.VMEM((CX * RIM, 256), F32)],
        compiler_params=PARAMS,
        cost_estimate=cost(10**9, 8 * 2**20),
    )(mix, face, hat, z_table, table)


def far(side, mix, face, hat, z_table, y_table, green):
    return pl.pallas_call(
        far_kernel,
        in_specs=[SMEM, SMEM] + [WHOLE] * 5,
        out_specs=WHOLE,
        out_shape=VOLUME,
        scratch_shapes=[pltpu.VMEM((2, RIM, N, N), F32)],
        compiler_params=PARAMS,
        cost_estimate=cost(4 * 10**9, 8 * 2**20),
    )(side, mix, face, hat, z_table, y_table, green)


def back(hat, field, wave, y_table, z_table):
    planes = 4
    volume = pl.BlockSpec((2, planes, N, N), lambda i: (0, i, 0, 0))
    return pl.pallas_call(
        back_kernel,
        grid=(CX // planes,),
        in_specs=[
            volume, volume, pl.BlockSpec((planes, N, N), lambda i: (i, 0, 0)),
            whole((2, 256, 256)), whole((2, 256, 256)),
        ],
        out_specs=volume,
        out_shape=VOLUME,
        compiler_params=PARAMS,
        cost_estimate=cost(6 * 10**9, 14 * 2**20),
    )(hat, field, wave, y_table, z_table)


def body(field, source, wave, coupling_x, coupling_y):
    n_gx = lax.axis_size("gx")
    n_gy = lax.axis_size("gy")
    gx = lax.axis_index("gx")
    gy = lax.axis_index("gy")
    odd = gx % 2
    near_pairs = [(i, i ^ 1) for i in range(n_gx)]
    far_pairs = [(i, ((i + 1) ^ 1) - 1) for i in range(1, n_gx - 1)]
    side_pairs = [(i, i ^ 1) for i in range(n_gy)]

    zf, zi, yf, yi = (jnp.asarray(t) for t in dft_tables())
    green = jnp.asarray(green_table())

    mix_low, mix_high = coupling_x[:, ::-1], coupling_x[::-1, :]
    mix_x = jnp.concatenate([mix_low, mix_high], axis=0)
    mix_far = jnp.where(odd == 1, mix_high, mix_low)
    sides = jnp.stack([odd, 1 - odd]).astype(F32)
    wide_low = jnp.broadcast_to(coupling_y[:, ::-1].T[:, :, None], (RIM, RIM, N))
    wide_high = jnp.broadcast_to(coupling_y[::-1, :].T[:, :, None], (RIM, RIM, N))
    mix_y = jnp.stack([wide_low, wide_high])
    mix_side = jnp.where(gy == 1, wide_low, wide_high)

    def rim_columns(offset):
        return jnp.concatenate(
            [yf[:, :, offset : offset + RIM], yf[:, :, N + offset : N + offset + RIM]], axis=2
        )

    side_table = jnp.where(gy == 1, rim_columns(0), rim_columns(N - RIM))

    for step in range(2):
        far_out = lax.dynamic_slice_in_dim(field, odd * (CX - RIM), RIM, axis=1)
        near_out = lax.dynamic_slice_in_dim(field, (1 - odd) * (CX - RIM), RIM, axis=1)
        side_out = lax.dynamic_slice_in_dim(field, (1 - gy) * (N - RIM), RIM, axis=2)
        far_in = lax.ppermute(far_out, "gx", far_pairs)
        near_in = lax.ppermute(near_out, "gx", near_pairs)
        side_in = lax.ppermute(side_out, "gy", side_pairs)
        hat = local(sides, mix_x, mix_y, field, source, wave, near_in, zf, yf)
        hat = add_side(mix_side, side_in, hat, zf, side_table)
        hat = far(sides, mix_far, far_in, hat, zf, yf, green)
        field = back(hat, field, wave, yi, zi)
    return field


def solution(mesh):
    placed = (P(None, "gx", "gy", None), P(None, "gx", "gy", None), P("gx", "gy", None), P(), P())
    return jax.shard_map(
        body, mesh=mesh, in_specs=placed, out_specs=P(None, "gx", "gy", None), check_vma=False
    )
```

```python
import functools
import math

import jax
import jax.numpy as jnp
import ml_dtypes
import numpy as np
from jax import lax
from jax.experimental import pallas as pl
from jax.experimental.pallas import tpu as pltpu
from jax.sharding import PartitionSpec as P

RIM = 8
HALF = 4
K0SQ = 2.4674
EPS = 2.5
CX = 32
N = 128
BF = jnp.bfloat16
F32 = jnp.float32
VMEM_LIMIT = 24 * 1024 * 1024


def two_halves(table):
    high = table.astype(ml_dtypes.bfloat16)
    low = (table - high.astype(np.float64)).astype(ml_dtypes.bfloat16)
    return np.stack([high, low])


def dft_tables():
    index = np.arange(N)
    angle = 2.0 * np.pi / N * (index[:, None] * index[None, :] % N)
    cosine, sine = np.cos(angle), np.sin(angle)
    z_forward = np.block([[cosine, -sine], [sine, cosine]])
    z_inverse = np.block([[cosine, sine], [-sine, cosine]])
    return (
        two_halves(z_forward),
        two_halves(z_inverse),
        two_halves(z_forward.T),
        two_halves(z_inverse.T),
    )


def side_tables(table):
    table = table.reshape(2, 2 * N, 2, N)
    return np.stack(
        [
            table[:, :, :, rows].reshape(2, 2 * N, 2 * RIM)
            for rows in (slice(0, RIM), slice(N - RIM, N))
        ]
    )


def angular_sq(length):
    freq = 2.0 * np.pi * np.fft.fftfreq(length)
    return freq * freq


def green_lines():
    table = green_table().astype(np.float64)
    both = np.concatenate([table, table[-2:0:-1]])
    lines = CX * np.fft.ifft(both[:, 0] + 1j * both[:, 1], axis=0)[:RIM]
    return np.stack([lines.real, lines.imag], axis=1).astype(np.float32)


def green_table():
    psq = (
        angular_sq(CX)[: CX // 2 + 1, None, None]
        + angular_sq(N)[None, :, None]
        + angular_sq(N)[None, None, :]
    )
    offset = psq - K0SQ
    denom = (offset * offset + EPS * EPS) * (CX * N * N)
    return np.stack([offset / denom, EPS / denom], axis=1).astype(np.float32)


def halves(value):
    high = value.astype(BF)
    return high, (value - high.astype(F32)).astype(BF)


def from_right(value, table):
    high, low = halves(value)
    out = jnp.dot(high, table[0], preferred_element_type=F32)
    out += jnp.dot(low, table[0], preferred_element_type=F32)
    return out + jnp.dot(high, table[1], preferred_element_type=F32)


def from_left(table, value):
    high, low = halves(value)
    out = jnp.dot(table[0], high, preferred_element_type=F32)
    out += jnp.dot(table[0], low, preferred_element_type=F32)
    return out + jnp.dot(table[1], high, preferred_element_type=F32)


def z_product(planes, table):
    count = planes[0][0].shape[0]
    tall = jnp.concatenate([jnp.concatenate([re, im], axis=1) for re, im in planes], axis=0)
    out = from_right(tall, table)
    parts = [out[k * count : (k + 1) * count] for k in range(len(planes))]
    return [(part[:, :N], part[:, N:]) for part in parts]


def y_product(planes, table):
    wide = jnp.concatenate(
        [jnp.concatenate([plane[part] for plane in planes], axis=1) for part in range(2)], axis=0
    )
    out = from_left(table, wide)
    parts = [out[:, k * N : (k + 1) * N] for k in range(len(planes))]
    return [(part[:N], part[N:]) for part in parts]


def transform(product, table, ref, count, group):
    def one(first):
        planes = [(ref[0, first + k], ref[1, first + k]) for k in range(group)]
        for k, (re, im) in enumerate(product(planes, table)):
            ref[0, first + k] = re
            ref[1, first + k] = im

    if count == group:
        one(0)
    else:
        pl.loop(0, count // group)(lambda i: one(i * group))


def times_root(value, step, length):
    re, im = value
    step %= length
    if step == 0:
        return value
    if 4 * step == length:
        return -im, re
    if 2 * step == length:
        return -re, -im
    if 4 * step == 3 * length:
        return im, -re
    c = math.cos(2.0 * math.pi * step / length)
    s = math.sin(2.0 * math.pi * step / length)
    if 8 * step % length == 0:
        h = math.sqrt(0.5)
        sc, ss = math.copysign(1.0, c), math.copysign(1.0, s)
        first = re - im if sc == ss else re + im
        second = re + im if sc == ss else im - re
        return first * (h * sc), second * (h * sc)
    return re * c - im * s, re * s + im * c


def fft(values, sign):
    count = len(values)
    if count == 1:
        return values
    even = fft(values[0::2], sign)
    odd = fft(values[1::2], sign)
    first, second = [], []
    for k in range(count // 2):
        re, im = times_root(odd[k], sign * k, count)
        first.append((even[k][0] + re, even[k][1] + im))
        second.append((even[k][0] - re, even[k][1] - im))
    return first + second


def fft_of_first(values, count):
    given = len(values)
    ratio = count // given
    out = [None] * count
    for k in range(ratio):
        turned = [times_root(value, -n * k, count) for n, value in enumerate(values)]
        out[k::ratio] = fft(turned, -1)
    return out


def filtered(spectrum, green, rows):
    scaled = []
    for k, (re, im) in enumerate(spectrum):
        g_re = green[min(k, CX - k), 0, rows, :]
        g_im = green[min(k, CX - k), 1, rows, :]
        scaled.append((re * g_re - im * g_im, re * g_im + im * g_re))
    return fft(scaled, 1)


def tiles(count, size):
    def wrap(step):
        pl.loop(0, count // size)(lambda t: step(pl.ds(pl.multiple_of(t * size, size), size)))

    return wrap


def mixed(mix_ref, row, first, source):
    total = mix_ref[row, first] * source[0]
    for r in range(1, len(source)):
        total += mix_ref[row, first + r] * source[r]
    return total


def cut_kernel(place_ref, field_ref, side_ref, first_ref, near_ref, second_ref, sems):
    far, near, rows = place_ref[0], place_ref[1], place_ref[2]
    rows = pl.multiple_of(rows, RIM)
    copies = [
        pltpu.make_async_copy(field_ref.at[:, :, pl.ds(rows, RIM), :], side_ref, sems.at[0]),
        pltpu.make_async_copy(field_ref.at[:, pl.ds(far, HALF)], first_ref, sems.at[1]),
        pltpu.make_async_copy(field_ref.at[:, pl.ds(far + HALF, HALF)], second_ref, sems.at[2]),
        pltpu.make_async_copy(field_ref.at[:, pl.ds(near, RIM)], near_ref, sems.at[3]),
    ]
    for copy in copies:
        copy.start()
    for copy in copies:
        copy.wait()


def by_depth(coupling_ref, side, b):
    rows = lax.broadcasted_iota(jnp.int32, (RIM, N), 0)
    column = jnp.zeros((RIM, N), F32)
    for a in range(RIM):
        value = coupling_ref[a, RIM - 1 - b] if side == 0 else coupling_ref[RIM - 1 - a, b]
        column = jnp.where(rows == a, value, column)
    return column


def spectrum_kernel(
    place_ref, x_ref, y_coupling_ref, planes_ref, z_ref, y_ref, mix_x_ref, mix_far_ref, mix_y_ref, out_ref
):
    odd = place_ref[0] > 0
    for a in range(RIM):
        for b in range(RIM):
            low, high = x_ref[a, RIM - 1 - b], x_ref[RIM - 1 - a, b]
            mix_x_ref[a, b] = low
            mix_x_ref[RIM + a, b] = high
            mix_far_ref[a, b] = jnp.where(odd, high, low)
    for side in range(2):
        for b in range(RIM):
            mix_y_ref[side, b] = by_depth(y_coupling_ref, side, b)
    planes = [(planes_ref[0, k], planes_ref[1, k]) for k in range(HALF)]
    for k, (re, im) in enumerate(y_product(z_product(planes, z_ref), y_ref)):
        out_ref[0, k] = re
        out_ref[1, k] = im


def local_kernel(
    side_ref, mix_x_ref, mix_y_ref, field_ref, source_ref, wave_ref, near_ref, z_ref, y_ref, after_ref,
    out_ref,
):
    @pl.loop(0, CX)
    def _(x):
        shifted = wave_ref[x] - K0SQ
        re, im = field_ref[0, x], field_ref[1, x]
        out_ref[0, x] = shifted * re + EPS * im + source_ref[0, x]
        out_ref[1, x] = shifted * im - EPS * re + source_ref[1, x]
        for part in range(2):
            first = field_ref[part, x, 0:RIM, :]
            last = field_ref[part, x, N - RIM : N, :]
            add_low = mix_y_ref[0, 0] * last[0:1]
            add_high = mix_y_ref[1, 0] * first[0:1]
            for b in range(1, RIM):
                add_low += mix_y_ref[0, b] * last[b : b + 1]
                add_high += mix_y_ref[1, b] * first[b : b + 1]
            out_ref[part, x, 0:RIM, :] += add_low
            out_ref[part, x, N - RIM : N, :] += add_high

    for side, base, other in ((0, 0, CX - RIM), (1, CX - RIM, 0)):
        weight = side_ref[side]

        @tiles(N, 16)
        def _(rows):
            for part in range(2):
                source = [
                    field_ref[part, other + r, rows, :] - weight * near_ref[part, r, rows, :]
                    for r in range(RIM)
                ]
                for p in range(RIM):
                    out_ref[part, base + p, rows, :] += mixed(mix_x_ref, side * RIM + p, 0, source)

    transform(z_product, z_ref, out_ref, CX, 16)
    transform(y_product, y_ref, out_ref, CX, 16)


def side_kernel(
    place_ref, mix_y_ref, face_ref, hat_ref, z_ref, table_ref, green_ref, out_ref, rows_ref, wide_ref
):
    upper = place_ref[3]
    mix_ref, table_ref = mix_y_ref.at[upper], table_ref.at[upper]

    @pl.loop(0, CX)
    def _(x):
        for part in range(2):
            tile = face_ref[part, x]
            total = mix_ref[0] * tile[0:1]
            for b in range(1, RIM):
                total += mix_ref[b] * tile[b : b + 1]
            rows_ref[pl.ds(pl.multiple_of(x * RIM, RIM), RIM), part * N : (part + 1) * N] = -total

    wide_ref[...] = from_right(rows_ref[...], z_ref)

    group = 8

    @pl.loop(0, CX // group)
    def _(i):
        rows = wide_ref[pl.ds(pl.multiple_of(i * group * RIM, group * RIM), group * RIM), :]
        parts = [rows[k * RIM : (k + 1) * RIM] for k in range(group)]
        short = [(part[:, :N], part[:, N:]) for part in parts]
        for k, (re, im) in enumerate(y_product(short, table_ref)):
            x = i * group + k
            out_ref[0, x] = hat_ref[0, x] + re
            out_ref[1, x] = hat_ref[1, x] + im

    @tiles(N, 8)
    def _(rows):
        given = [(out_ref[0, x, rows, :], out_ref[1, x, rows, :]) for x in range(CX)]
        for x, (re, im) in enumerate(filtered(fft(given, -1), green_ref, rows)):
            out_ref[0, x, rows, :] = re
            out_ref[1, x, rows, :] = im


def first_kernel(mix_ref, face_ref, z_ref, y_ref, after_ref, out_ref):
    @tiles(N, 16)
    def _(rows):
        for part in range(2):
            source = [face_ref[part, r, rows, :] for r in range(HALF)]
            for p in range(RIM):
                out_ref[part, p, rows, :] = -mixed(mix_ref, p, 0, source)

    transform(z_product, z_ref, out_ref, RIM, RIM)
    transform(y_product, y_ref, out_ref, RIM, RIM)


def damped(re, im, back, wave):
    ratio = (wave - K0SQ) * (1.0 / EPS)
    r_re, r_im = re - back[0], im - back[1]
    return re - (r_re - ratio * r_im), im - (r_im + ratio * r_re)


def early_kernel(
    place_ref, mix_ref, second_ref, first_ref, part_ref, line_ref, field_ref, wave_ref, y_ref, z_ref,
    hat_ref, out_ref, work_ref,
):
    base = place_ref[0]

    @tiles(N, 8)
    def _(rows):
        for part in range(2):
            source = [second_ref[part, r, rows, :] for r in range(HALF)]
            for p in range(RIM):
                hat_ref[part, p, rows, :] = first_ref[part, p, rows, :] - mixed(
                    mix_ref, p, HALF, source
                )

    @tiles(N, 8)
    def _(rows):
        given = [(hat_ref[0, p, rows, :], hat_ref[1, p, rows, :]) for p in range(RIM)]
        lines = [(line_ref[d, 0, rows, :], line_ref[d, 1, rows, :]) for d in range(RIM)]
        for p in range(HALF):
            re = part_ref[0, base + p, rows, :]
            im = part_ref[1, base + p, rows, :]
            for q, (t_re, t_im) in enumerate(given):
                g_re, g_im = lines[abs(p - q)]
                re += t_re * g_re - t_im * g_im
                im += t_re * g_im + t_im * g_re
            work_ref[0, p, rows, :] = re
            work_ref[1, p, rows, :] = im

    planes = [(work_ref[0, k], work_ref[1, k]) for k in range(HALF)]
    for k, back in enumerate(z_product(y_product(planes, y_ref), z_ref)):
        re, im = damped(field_ref[0, base + k], field_ref[1, base + k], back, wave_ref[base + k])
        out_ref[0, k] = re
        out_ref[1, k] = im


def filter_far(base, given_of, part_ref, green_ref, work_ref):
    @tiles(N, 8)
    def _(rows):
        spectrum = fft_of_first(given_of(rows), CX)
        for k, (re, im) in enumerate(filtered(spectrum, green_ref, rows)):
            x = lax.rem(base + k, CX)
            work_ref[0, x, rows, :] = part_ref[0, x, rows, :] + re
            work_ref[1, x, rows, :] = part_ref[1, x, rows, :] + im


def step_back(work_ref, field_ref, wave_ref, y_ref, z_ref, out_ref):
    group = 16
    transform(y_product, y_ref, work_ref, CX, group)

    @pl.loop(0, CX // group)
    def _(i):
        first = i * group
        planes = [(work_ref[0, first + k], work_ref[1, first + k]) for k in range(group)]
        for k, back in enumerate(z_product(planes, z_ref)):
            x = first + k
            re, im = damped(field_ref[0, x], field_ref[1, x], back, wave_ref[x])
            out_ref[0, x] = re
            out_ref[1, x] = im


def middle_kernel(
    place_ref, hat_ref, part_ref, green_ref, field_ref, wave_ref, yi_ref, zi_ref, z_ref, y_ref,
    out_ref, side_ref, near_ref, second_ref, work_ref,
):
    base = place_ref[0]

    def given_of(rows):
        return [(hat_ref[0, p, rows, :], hat_ref[1, p, rows, :]) for p in range(RIM)]

    filter_far(base, given_of, part_ref, green_ref, work_ref)
    step_back(work_ref, field_ref, wave_ref, yi_ref, zi_ref, out_ref)

    cut = pl.ds(pl.multiple_of(place_ref[2], RIM), RIM)
    for part in range(2):
        side_ref[part] = out_ref[part, :, cut, :]
        near_ref[part] = out_ref[part, pl.ds(place_ref[1], RIM)]
    planes = [(out_ref[0, base + k], out_ref[1, base + k]) for k in range(HALF, RIM)]
    for k, (re, im) in enumerate(y_product(z_product(planes, z_ref), y_ref)):
        second_ref[0, k] = re
        second_ref[1, k] = im


def last_kernel(
    place_ref, mix_ref, second_ref, first_ref, part_ref, green_ref, field_ref, wave_ref, yi_ref, zi_ref,
    out_ref, work_ref, done_ref, sems,
):
    def given_of(rows):
        sums = []
        for part in range(2):
            source = [second_ref[part, r, rows, :] for r in range(HALF)]
            sums.append(
                [
                    first_ref[part, p, rows, :] - mixed(mix_ref, p, HALF, source)
                    for p in range(RIM)
                ]
            )
        return list(zip(*sums))

    filter_far(place_ref[0], given_of, part_ref, green_ref, work_ref)
    transform(y_product, yi_ref, work_ref, CX, 16)
    copies = []
    for i, (first, group) in enumerate(((0, 16), (16, 8), (24, 8))):
        planes = [(work_ref[0, first + k], work_ref[1, first + k]) for k in range(group)]
        for k, back in enumerate(z_product(planes, zi_ref)):
            x = first + k
            re, im = damped(field_ref[0, x], field_ref[1, x], back, wave_ref[x])
            done_ref[0, x] = re
            done_ref[1, x] = im
        span = pl.ds(first, group)
        copies.append(pltpu.make_async_copy(done_ref.at[:, span], out_ref.at[:, span], sems.at[i]))
        copies[-1].start()
    for copy in copies:
        copy.wait()


SMEM = pl.BlockSpec(memory_space=pltpu.SMEM)
WHOLE = pl.BlockSpec(memory_space=pltpu.VMEM)


def array(*shape):
    return jax.ShapeDtypeStruct(shape, F32)


VOLUME = array(2, CX, N, N)
FACE = array(2, RIM, N, N)
PART = array(2, HALF, N, N)
SIDE = array(2, CX, RIM, N)


PARAMS = pltpu.CompilerParams(vmem_limit_bytes=VMEM_LIMIT)


def cost(weight):
    return pl.CostEstimate(flops=weight * 10**9, bytes_accessed=weight * 10**6, transcendentals=0)


COST = cost(1)


def call(kernel, scalars, operands, out, scratch=(), after=None, weight=1):
    later = [] if after is None else [after]
    return pl.pallas_call(
        kernel,
        in_specs=[SMEM] * len(scalars) + [WHOLE] * len(operands)
        + [pl.BlockSpec(memory_space=pl.ANY)] * len(later),
        out_specs=jax.tree.map(lambda _: WHOLE, out),
        out_shape=out,
        scratch_shapes=[pltpu.VMEM(s.shape, s.dtype) for s in scratch],
        compiler_params=PARAMS,
        cost_estimate=cost(weight),
    )(*scalars, *operands, *later)


def prepare(place, coupling_x, coupling_y, planes, z_table, y_table):
    return pl.pallas_call(
        spectrum_kernel,
        in_specs=[SMEM] * 3 + [WHOLE] * 3,
        out_specs=(SMEM, SMEM, WHOLE, WHOLE),
        out_shape=(array(2 * RIM, RIM), array(RIM, RIM), array(2, RIM, RIM, N), PART),
        compiler_params=PARAMS,
        cost_estimate=COST,
    )(place, coupling_x, coupling_y, planes, z_table, y_table)


def cut_faces(place, field):
    out = (SIDE, PART, FACE, PART)
    return pl.pallas_call(
        cut_kernel,
        in_specs=[SMEM, pl.BlockSpec(memory_space=pltpu.HBM)],
        out_specs=(WHOLE,) * 4,
        out_shape=out,
        scratch_shapes=[pltpu.SemaphoreType.DMA((4,))],
        compiler_params=PARAMS,
        cost_estimate=COST,
    )(place, field)


def body(field, source, wave, coupling_x, coupling_y):
    n_gx = lax.axis_size("gx")
    n_gy = lax.axis_size("gy")
    gx = lax.axis_index("gx")
    gy = lax.axis_index("gy")
    odd = gx % 2
    near_pairs = [(i, i ^ 1) for i in range(n_gx)]
    far_pairs = [(i, ((i + 1) ^ 1) - 1) for i in range(1, n_gx - 1)]
    side_pairs = [(i, i ^ 1) for i in range(n_gy)]

    zf, zi, yf, yi = (jnp.asarray(t) for t in dft_tables())
    green = jnp.asarray(green_table())
    lines = jnp.asarray(green_lines())

    weights = jnp.stack([odd, 1 - odd]).astype(F32)
    span = CX - RIM
    place = jnp.stack([odd * span, (1 - odd) * span, (1 - gy) * (N - RIM), 1 - gy]).astype(jnp.int32)
    rims = side_tables(dft_tables()[2])

    side_out, first_out, near_out, second_raw = cut_faces(place, field)
    mix_x, mix_far, mix_y, second_out = prepare(place, coupling_x, coupling_y, second_raw, zf, yf)
    for step in range(2):
        side_in = lax.ppermute(side_out, "gy", side_pairs)
        first_in = lax.ppermute(first_out, "gx", far_pairs)
        near_in = lax.ppermute(near_out, "gx", near_pairs)
        second_in = lax.ppermute(second_out, "gx", far_pairs)
        rows = array(CX * RIM, 2 * N)

        def far_part(after):
            return call(
                first_kernel, (mix_far,), (first_in, zf, yf), FACE, after=after,
                weight=10 if step == 0 else 60,
            )

        first = far_part(place) if step == 1 else None
        hat = call(
            local_kernel, (weights, mix_x), (mix_y, field, source, wave, near_in, zf, yf), VOLUME,
            after=place if first is None else first, weight=5,
        )
        part = call(
            side_kernel, (place,), (mix_y, side_in, hat, zf, rims, green), VOLUME, (rows, rows), weight=30
        )
        if first is None:
            first = far_part(part)
        if step == 0:
            whole, first_out = call(
                early_kernel, (place, mix_far),
                (second_in, first, part, lines, field, wave, yi, zi), (FACE, PART), (PART,),
            )
            field, side_out, near_out, second_out = call(
                middle_kernel, (place,), (whole, part, green, field, wave, yi, zi, zf, yf),
                (VOLUME, SIDE, FACE, PART), (VOLUME,),
            )
        else:
            field = pl.pallas_call(
                last_kernel,
                in_specs=[SMEM] * 2 + [WHOLE] * 8,
                out_specs=pl.BlockSpec(memory_space=pltpu.HBM),
                out_shape=VOLUME,
                scratch_shapes=[
                    pltpu.VMEM(VOLUME.shape, F32),
                    pltpu.VMEM(VOLUME.shape, F32),
                    pltpu.SemaphoreType.DMA((3,)),
                ],
                compiler_params=PARAMS,
                cost_estimate=COST,
            )(place, mix_far, second_in, first, part, green, field, wave, yi, zi)
    return field


def solution(mesh):
    placed = (P(None, "gx", "gy", None), P(None, "gx", "gy", None), P("gx", "gy", None), P(), P())
    return jax.shard_map(
        body, mesh=mesh, in_specs=placed, out_specs=P(None, "gx", "gy", None), check_vma=False
    )
```

```python
import functools
import math

import jax
import jax.numpy as jnp
import numpy as np
from jax import lax
from jax.experimental import pallas as pl
from jax.experimental.pallas import tpu as pltpu
from jax.sharding import PartitionSpec as P

RIM = 8
LEAD = 3
REST = RIM - LEAD
RING = 4
K0SQ = 2.4674
EPS = 2.5
CX = 32
N = 128
BF = jnp.bfloat16
F32 = jnp.float32
VMEM_LIMIT = 24 * 1024 * 1024


def dft_tables():
    index = np.arange(N)
    angle = 2.0 * np.pi / N * (index[:, None] * index[None, :] % N)
    cosine, sine = np.cos(angle), np.sin(angle)
    forward = np.block([[cosine, -sine], [sine, cosine]])
    inverse = np.block([[cosine, sine], [-sine, cosine]])
    return forward, inverse


def angular_sq(length):
    freq = 2.0 * np.pi * np.fft.fftfreq(length)
    return freq * freq


def green_lines():
    table = green_table().astype(np.float64)
    both = np.concatenate([table, table[-2:0:-1]])
    lines = CX * np.fft.ifft(both[:, 0] + 1j * both[:, 1], axis=0)[:RIM]
    return np.stack([lines.real, lines.imag], axis=1).astype(np.float32)


def green_table():
    psq = (
        angular_sq(CX)[: CX // 2 + 1, None, None]
        + angular_sq(N)[None, :, None]
        + angular_sq(N)[None, None, :]
    )
    offset = psq - K0SQ
    denom = (offset * offset + EPS * EPS) * (CX * N * N)
    return np.stack([offset / denom, EPS / denom], axis=1).astype(np.float32)


def halves(value):
    high = value.astype(BF)
    return high, (value - high.astype(F32)).astype(BF)


def from_right(value, table):
    high, low = halves(value)
    out = jnp.dot(high, table[0], preferred_element_type=F32)
    out += jnp.dot(low, table[0], preferred_element_type=F32)
    return out + jnp.dot(high, table[1], preferred_element_type=F32)


def from_left(table, value):
    high, low = halves(value)
    out = jnp.dot(table[0], high, preferred_element_type=F32)
    out += jnp.dot(table[0], low, preferred_element_type=F32)
    return out + jnp.dot(table[1], high, preferred_element_type=F32)


def z_product(planes, table):
    count = planes[0][0].shape[0]
    tall = jnp.concatenate([jnp.concatenate([re, im], axis=1) for re, im in planes], axis=0)
    out = from_right(tall, table)
    parts = [out[k * count : (k + 1) * count] for k in range(len(planes))]
    return [(part[:, :N], part[:, N:]) for part in parts]


def y_product(planes, table):
    wide = jnp.concatenate(
        [jnp.concatenate([plane[part] for plane in planes], axis=1) for part in range(2)], axis=0
    )
    out = from_left(table, wide)
    parts = [out[:, k * N : (k + 1) * N] for k in range(len(planes))]
    return [(part[:N], part[N:]) for part in parts]


def transform(product, table, ref, count, group):
    def one(first):
        planes = [(ref[0, first + k], ref[1, first + k]) for k in range(group)]
        for k, (re, im) in enumerate(product(planes, table)):
            ref[0, first + k] = re
            ref[1, first + k] = im

    if count == group:
        one(0)
    else:
        pl.loop(0, count // group)(lambda i: one(i * group))


def times_root(value, step, length):
    re, im = value
    step %= length
    if step == 0:
        return value
    if 4 * step == length:
        return -im, re
    if 2 * step == length:
        return -re, -im
    if 4 * step == 3 * length:
        return im, -re
    c = math.cos(2.0 * math.pi * step / length)
    s = math.sin(2.0 * math.pi * step / length)
    if 8 * step % length == 0:
        h = math.sqrt(0.5)
        sc, ss = math.copysign(1.0, c), math.copysign(1.0, s)
        first = re - im if sc == ss else re + im
        second = re + im if sc == ss else im - re
        return first * (h * sc), second * (h * sc)
    return re * c - im * s, re * s + im * c


def fft(values, sign):
    count = len(values)
    if count == 1:
        return values
    even = fft(values[0::2], sign)
    odd = fft(values[1::2], sign)
    first, second = [], []
    for k in range(count // 2):
        re, im = times_root(odd[k], sign * k, count)
        first.append((even[k][0] + re, even[k][1] + im))
        second.append((even[k][0] - re, even[k][1] - im))
    return first + second


def fft_of_first(values, count):
    given = len(values)
    ratio = count // given
    out = [None] * count
    for k in range(ratio):
        turned = [times_root(value, -n * k, count) for n, value in enumerate(values)]
        out[k::ratio] = fft(turned, -1)
    return out


def filtered(spectrum, green, rows):
    scaled = []
    for k, (re, im) in enumerate(spectrum):
        g_re = green[min(k, CX - k), 0, rows, :]
        g_im = green[min(k, CX - k), 1, rows, :]
        scaled.append((re * g_re - im * g_im, re * g_im + im * g_re))
    return fft(scaled, 1)


def tiles(count, size):
    def wrap(step):
        pl.loop(0, count // size)(lambda t: step(pl.ds(pl.multiple_of(t * size, size), size)))

    return wrap


def mixed(mix_ref, row, first, source):
    total = mix_ref[row, first] * source[0]
    for r in range(1, len(source)):
        total += mix_ref[row, first + r] * source[r]
    return total


def cut_kernel(place_ref, field_ref, side_ref, first_ref, near_ref, sems):
    far, near, rows = place_ref[0], place_ref[1], pl.multiple_of(place_ref[2], RIM)
    copies = [
        pltpu.make_async_copy(field_ref.at[:, :, pl.ds(rows, RIM), :], side_ref, sems.at[0]),
        pltpu.make_async_copy(field_ref.at[:, pl.ds(far, LEAD)], first_ref, sems.at[1]),
        pltpu.make_async_copy(field_ref.at[:, pl.ds(near, RIM)], near_ref, sems.at[2]),
    ]
    for copy in copies:
        copy.start()
    for copy in copies:
        copy.wait()


def by_depth(coupling_ref, side, b):
    rows = lax.broadcasted_iota(jnp.int32, (RIM, N), 0)
    column = jnp.zeros((RIM, N), F32)
    for a in range(RIM):
        value = coupling_ref[a, RIM - 1 - b] if side == 0 else coupling_ref[RIM - 1 - a, b]
        column = jnp.where(rows == a, value, column)
    return column


def spectrum_kernel(
    place_ref, x_ref, y_coupling_ref, field_ref, forward_ref, inverse_ref, after_ref,
    mix_x_ref, mix_far_ref, mix_y_ref, out_ref, z_ref, y_ref, planes_ref, sem,
):
    far = place_ref[0]
    copy = pltpu.make_async_copy(field_ref.at[:, pl.ds(far + LEAD, REST)], planes_ref, sem)
    copy.start()
    odd = far > 0
    for a in range(RIM):
        for b in range(RIM):
            low, high = x_ref[a, RIM - 1 - b], x_ref[RIM - 1 - a, b]
            mix_x_ref[a, b] = low
            mix_x_ref[RIM + a, b] = high
            mix_far_ref[a, b] = jnp.where(odd, high, low)
    for table_ref, halves_ref in ((forward_ref, z_ref), (inverse_ref, y_ref)):
        halves_ref[0], halves_ref[1] = halves(table_ref[...])
    for side in range(2):
        for b in range(RIM):
            mix_y_ref[side, b] = by_depth(y_coupling_ref, side, b)
    copy.wait()
    planes = [(planes_ref[0, k], planes_ref[1, k]) for k in range(REST)]
    for k, (re, im) in enumerate(y_product(z_product(planes, z_ref), y_ref)):
        out_ref[0, k] = re
        out_ref[1, k] = im


def local_kernel(
    side_ref, place_ref, mix_x_ref, mix_y_ref, field_ref, source_ref, wave_ref, near_ref, z_ref,
    after_ref, out_ref,
):
    base = place_ref[0]

    @pl.loop(0, CX)
    def _(x):
        shifted = wave_ref[x] - K0SQ
        re, im = field_ref[0, x], field_ref[1, x]
        to = lax.rem(x + CX - base, CX)
        out_ref[0, to] = shifted * re + EPS * im + source_ref[0, x]
        out_ref[1, to] = shifted * im - EPS * re + source_ref[1, x]
        for part in range(2):
            first = field_ref[part, x, 0:RIM, :]
            last = field_ref[part, x, N - RIM : N, :]
            add_low = mix_y_ref[0, 0] * last[0:1]
            add_high = mix_y_ref[1, 0] * first[0:1]
            for b in range(1, RIM):
                add_low += mix_y_ref[0, b] * last[b : b + 1]
                add_high += mix_y_ref[1, b] * first[b : b + 1]
            out_ref[part, to, 0:RIM, :] += add_low
            out_ref[part, to, N - RIM : N, :] += add_high

    for side, start, other in ((0, 0, CX - RIM), (1, CX - RIM, 0)):
        weight = side_ref[side]
        to = lax.rem(start + CX - base, CX)

        @tiles(N, 16)
        def _(rows):
            for part in range(2):
                source = [
                    field_ref[part, other + r, rows, :] - weight * near_ref[part, r, rows, :]
                    for r in range(RIM)
                ]
                for p in range(RIM):
                    out_ref[part, to + p, rows, :] += mixed(mix_x_ref, side * RIM + p, 0, source)

    transform(z_product, z_ref, out_ref, CX, 16)


def side_kernel(
    side_ref, place_ref, mix_y_ref, face_ref, hat_ref, z_ref, y_ref, green_ref, out_ref, rows_ref, wide_ref
):
    mix_ref = mix_y_ref.at[place_ref[3]]

    @pl.loop(0, CX)
    def _(x):
        for part in range(2):
            tile = face_ref[part, lax.rem(x + place_ref[0], CX)]
            total = mix_ref[0] * tile[0:1]
            for b in range(1, RIM):
                total += mix_ref[b] * tile[b : b + 1]
            rows_ref[pl.ds(pl.multiple_of(x * RIM, RIM), RIM), part * N : (part + 1) * N] = -total

    wide_ref[...] = from_right(rows_ref[...], z_ref)
    low, high = side_ref[2], side_ref[3]
    group = 16

    def with_side(part, x, term):
        value = hat_ref[part, x]
        return jnp.concatenate(
            [value[:RIM] + low * term, value[RIM : N - RIM], value[N - RIM :] + high * term], axis=0
        )

    @pl.loop(0, CX // group)
    def _(i):
        terms = wide_ref[pl.ds(pl.multiple_of(i * group * RIM, group * RIM), group * RIM), :]
        planes = []
        for k in range(group):
            term = terms[k * RIM : (k + 1) * RIM]
            x = i * group + k
            planes.append((with_side(0, x, term[:, :N]), with_side(1, x, term[:, N:])))
        for k, (re, im) in enumerate(y_product(planes, y_ref)):
            out_ref[0, i * group + k] = re
            out_ref[1, i * group + k] = im

    @tiles(N, 8)
    def _(rows):
        given = [(out_ref[0, x, rows, :], out_ref[1, x, rows, :]) for x in range(CX)]
        for x, (re, im) in enumerate(filtered(fft(given, -1), green_ref, rows)):
            out_ref[0, x, rows, :] = re
            out_ref[1, x, rows, :] = im


def first_kernel(mix_ref, face_ref, z_ref, y_ref, after_ref, out_ref):
    @tiles(N, 16)
    def _(rows):
        for part in range(2):
            source = [face_ref[part, r, rows, :] for r in range(LEAD)]
            for p in range(RIM):
                out_ref[part, p, rows, :] = -mixed(mix_ref, p, 0, source)

    transform(z_product, z_ref, out_ref, RIM, RIM)
    transform(y_product, y_ref, out_ref, RIM, RIM)


def damped(re, im, back, wave):
    ratio = (wave - K0SQ) * (1.0 / EPS)
    r_re, r_im = re - back[0], im - back[1]
    return re - (r_re - ratio * r_im), im - (r_im + ratio * r_re)


def early_kernel(
    place_ref, mix_ref, second_ref, first_ref, part_ref, line_ref, field_ref, wave_ref, y_ref, z_ref,
    hat_ref, out_ref, work_ref,
):
    base = place_ref[0]

    @tiles(N, 8)
    def _(rows):
        for part in range(2):
            source = [second_ref[part, r, rows, :] for r in range(REST)]
            for p in range(RIM):
                hat_ref[part, p, rows, :] = first_ref[part, p, rows, :] - mixed(
                    mix_ref, p, LEAD, source
                )

    @tiles(N, 8)
    def _(rows):
        given = [(hat_ref[0, p, rows, :], hat_ref[1, p, rows, :]) for p in range(RIM)]
        lines = [(line_ref[d, 0, rows, :], line_ref[d, 1, rows, :]) for d in range(RIM)]
        for p in range(LEAD):
            re = part_ref[0, p, rows, :]
            im = part_ref[1, p, rows, :]
            for q, (t_re, t_im) in enumerate(given):
                g_re, g_im = lines[abs(p - q)]
                re += t_re * g_re - t_im * g_im
                im += t_re * g_im + t_im * g_re
            work_ref[0, p, rows, :] = re
            work_ref[1, p, rows, :] = im

    planes = [(work_ref[0, k], work_ref[1, k]) for k in range(LEAD)]
    for k, back in enumerate(z_product(y_product(planes, y_ref), z_ref)):
        re, im = damped(field_ref[0, base + k], field_ref[1, base + k], back, wave_ref[base + k])
        out_ref[0, k] = re
        out_ref[1, k] = im


def filter_far(given_of, part_ref, green_ref, z_ref, ring_refs, work_ref):
    ring = len(ring_refs)

    @pl.loop(0, N // (8 * ring))
    def _(i):
        for j, ring_ref in enumerate(ring_refs):
            rows = pl.ds(pl.multiple_of(i * 8 * ring, 8 * ring) + 8 * j, 8)
            spectrum = fft_of_first(given_of(rows), CX)
            for x, (re, im) in enumerate(filtered(spectrum, green_ref, rows)):
                ring_ref[0, x] = part_ref[0, x, rows, :] + re
                ring_ref[1, x] = part_ref[1, x, rows, :] + im
            planes = [(ring_ref[0, x], ring_ref[1, x]) for x in range(CX)]
            for x, (re, im) in enumerate(z_product(planes, z_ref)):
                work_ref[0, x, rows, :] = re
                work_ref[1, x, rows, :] = im


def step_back(base, first, group, work_ref, field_ref, wave_ref, y_ref, out_ref):
    planes = [(work_ref[0, first + k], work_ref[1, first + k]) for k in range(group)]
    for k, back in enumerate(y_product(planes, y_ref)):
        x = lax.rem(first + k + base, CX)
        re, im = damped(field_ref[0, x], field_ref[1, x], back, wave_ref[x])
        out_ref[0, x] = re
        out_ref[1, x] = im


def middle_kernel(
    place_ref, hat_ref, part_ref, green_ref, field_ref, wave_ref, yi_ref, zi_ref, z_ref, y_ref,
    out_ref, side_ref, near_ref, second_ref, work_ref, *ring_refs,
):
    base = place_ref[0]

    def given_of(rows):
        return [(hat_ref[0, p, rows, :], hat_ref[1, p, rows, :]) for p in range(RIM)]

    filter_far(given_of, part_ref, green_ref, zi_ref, ring_refs, work_ref)
    for first in (0, 16):
        step_back(base, first, 16, work_ref, field_ref, wave_ref, yi_ref, out_ref)

    cut = pl.ds(pl.multiple_of(place_ref[2], RIM), RIM)
    for part in range(2):
        side_ref[part] = out_ref[part, :, cut, :]
        near_ref[part] = out_ref[part, pl.ds(place_ref[1], RIM)]
    planes = [(out_ref[0, base + k], out_ref[1, base + k]) for k in range(LEAD, RIM)]
    for k, (re, im) in enumerate(y_product(z_product(planes, z_ref), y_ref)):
        second_ref[0, k] = re
        second_ref[1, k] = im


def last_kernel(
    place_ref, mix_ref, second_ref, first_ref, part_ref, green_ref, field_ref, wave_ref, yi_ref, zi_ref,
    out_ref, work_ref, done_ref, sems, *ring_refs,
):
    def given_of(rows):
        sums = []
        for part in range(2):
            source = [second_ref[part, r, rows, :] for r in range(REST)]
            sums.append(
                [first_ref[part, p, rows, :] - mixed(mix_ref, p, LEAD, source) for p in range(RIM)]
            )
        return list(zip(*sums))

    base = place_ref[0]
    filter_far(given_of, part_ref, green_ref, zi_ref, ring_refs, work_ref)
    copies = []
    for first in range(0, CX, RIM):
        step_back(base, first, RIM, work_ref, field_ref, wave_ref, yi_ref, done_ref)
        span = pl.ds(lax.rem(base + first, CX), RIM)
        sem = sems.at[first // RIM]
        copies.append(pltpu.make_async_copy(done_ref.at[:, span], out_ref.at[:, span], sem))
        copies[-1].start()
    for copy in copies:
        copy.wait()


SMEM = pl.BlockSpec(memory_space=pltpu.SMEM)
WHOLE = pl.BlockSpec(memory_space=pltpu.VMEM)


def array(*shape):
    return jax.ShapeDtypeStruct(shape, F32)


VOLUME = array(2, CX, N, N)
FACE = array(2, RIM, N, N)
PART = array(2, LEAD, N, N)
OTHER = array(2, REST, N, N)
SIDE = array(2, CX, RIM, N)
RINGS = (array(2, CX, 8, N),) * RING


PARAMS = pltpu.CompilerParams(vmem_limit_bytes=VMEM_LIMIT)


def cost(weight):
    return pl.CostEstimate(flops=weight * 10**9, bytes_accessed=weight * 10**6, transcendentals=0)


COST = cost(1)


def call(kernel, scalars, operands, out, scratch=(), after=None, weight=1):
    later = [] if after is None else [after]
    return pl.pallas_call(
        kernel,
        in_specs=[SMEM] * len(scalars) + [WHOLE] * len(operands)
        + [pl.BlockSpec(memory_space=pl.ANY)] * len(later),
        out_specs=jax.tree.map(lambda _: WHOLE, out),
        out_shape=out,
        scratch_shapes=[pltpu.VMEM(s.shape, s.dtype) for s in scratch],
        compiler_params=PARAMS,
        cost_estimate=cost(weight),
    )(*scalars, *operands, *later)


HBM = pl.BlockSpec(memory_space=pltpu.HBM)


def prepare(place, coupling_x, coupling_y, field, forward, inverse, after):
    table = jax.ShapeDtypeStruct((2, 2 * N, 2 * N), BF)
    return pl.pallas_call(
        spectrum_kernel,
        in_specs=[SMEM] * 3 + [HBM] + [WHOLE] * 2 + [pl.BlockSpec(memory_space=pl.ANY)],
        out_specs=(SMEM,) * 2 + (WHOLE,) * 4,
        out_shape=(
            array(2 * RIM, RIM), array(RIM, RIM), array(2, RIM, RIM, N), OTHER, table, table
        ),
        scratch_shapes=[pltpu.VMEM(OTHER.shape, F32), pltpu.SemaphoreType.DMA],
        compiler_params=PARAMS,
        cost_estimate=COST,
    )(place, coupling_x, coupling_y, field, forward, inverse, after)


def cut_faces(place, field):
    return pl.pallas_call(
        cut_kernel,
        in_specs=[SMEM, HBM],
        out_specs=(WHOLE,) * 3,
        out_shape=(SIDE, PART, FACE),
        scratch_shapes=[pltpu.SemaphoreType.DMA((3,))],
        compiler_params=PARAMS,
        cost_estimate=COST,
    )(place, field)


def body(field, source, wave, coupling_x, coupling_y):
    n_gx = lax.axis_size("gx")
    n_gy = lax.axis_size("gy")
    gx = lax.axis_index("gx")
    gy = lax.axis_index("gy")
    odd = gx % 2
    near_pairs = [(i, i ^ 1) for i in range(n_gx)]
    far_pairs = [(i, ((i + 1) ^ 1) - 1) for i in range(1, n_gx - 1)]
    side_pairs = [(i, i ^ 1) for i in range(n_gy)]

    forward, inverse = (jnp.asarray(t, F32) for t in dft_tables())
    green = jnp.asarray(green_table())
    lines = jnp.asarray(green_lines())

    weights = jnp.stack([odd, 1 - odd, gy, 1 - gy]).astype(F32)
    span = CX - RIM
    place = jnp.stack([odd * span, (1 - odd) * span, (1 - gy) * (N - RIM), 1 - gy]).astype(jnp.int32)
    pinned = pltpu.with_memory_space_constraint(field, pltpu.HBM)
    side_out, first_out, near_out = cut_faces(place, pinned)
    mix_x, mix_far, mix_y, second_out, zf, zi = prepare(
        place, coupling_x, coupling_y, pinned, forward, inverse, first_out
    )
    yf, yi = zi, zf
    for step in range(2):
        side_in = lax.ppermute(side_out, "gy", side_pairs)
        first_in = lax.ppermute(first_out, "gx", far_pairs)
        near_in = lax.ppermute(near_out, "gx", near_pairs)
        second_in = lax.ppermute(second_out, "gx", far_pairs)
        rows = array(CX * RIM, 2 * N)

        def far_part(after):
            return call(
                first_kernel, (mix_far,), (first_in, zf, yf), FACE, after=after, weight=60
            )

        first = far_part(place) if step == 1 else None
        hat = call(
            local_kernel, (weights, place, mix_x), (mix_y, field, source, wave, near_in, zf), VOLUME,
            after=place if first is None else first,
        )
        part = call(
            side_kernel, (weights, place), (mix_y, side_in, hat, zf, yf, green), VOLUME, (rows, rows),
            weight=30,
        )
        if first is None:
            first = far_part(part)
        if step == 0:
            whole, first_out = call(
                early_kernel, (place, mix_far),
                (second_in, first, part, lines, field, wave, yi, zi), (FACE, PART), (PART,),
            )
            field, side_out, near_out, second_out = call(
                middle_kernel, (place,), (whole, part, green, field, wave, yi, zi, zf, yf),
                (VOLUME, SIDE, FACE, OTHER), (VOLUME, *RINGS),
            )
        else:
            field = pl.pallas_call(
                last_kernel,
                in_specs=[SMEM] * 2 + [WHOLE] * 8,
                out_specs=pl.BlockSpec(memory_space=pltpu.HBM),
                out_shape=VOLUME,
                scratch_shapes=[
                    pltpu.VMEM(VOLUME.shape, F32),
                    pltpu.VMEM(VOLUME.shape, F32),
                    pltpu.SemaphoreType.DMA((CX // RIM,)),
                    *(pltpu.VMEM(r.shape, F32) for r in RINGS),
                ],
                compiler_params=PARAMS,
                cost_estimate=COST,
            )(place, mix_far, second_in, first, part, green, field, wave, yi, zi)
    return field


def solution(mesh):
    placed = (P(None, "gx", "gy", None), P(None, "gx", "gy", None), P("gx", "gy", None), P(), P())
    return jax.shard_map(
        body, mesh=mesh, in_specs=placed, out_specs=P(None, "gx", "gy", None), check_vma=False
    )
```

```python
import functools
import math

import jax
import jax.numpy as jnp
import numpy as np
from jax import lax
from jax.experimental import pallas as pl
from jax.experimental.pallas import tpu as pltpu
from jax.sharding import PartitionSpec as P

RIM = 8
LEAD = 3
REST = RIM - LEAD
RING = 8
K0SQ = 2.4674
EPS = 2.5
CX = 32
N = 128
BF = jnp.bfloat16
F32 = jnp.float32
VMEM_LIMIT = 24 * 1024 * 1024


def dft_tables():
    index = np.arange(N)
    angle = 2.0 * np.pi / N * (index[:, None] * index[None, :] % N)
    cosine, sine = np.cos(angle), np.sin(angle)
    forward = np.block([[cosine, -sine], [sine, cosine]])
    inverse = np.block([[cosine, sine], [-sine, cosine]])
    return forward, inverse


def angular_sq(length):
    freq = 2.0 * np.pi * np.fft.fftfreq(length)
    return freq * freq


def green_lines():
    table = green_table().astype(np.float64)
    both = np.concatenate([table, table[-2:0:-1]])
    lines = CX * np.fft.ifft(both[:, 0] + 1j * both[:, 1], axis=0)[:RIM]
    return np.stack([lines.real, lines.imag], axis=1).astype(np.float32)


def green_table():
    psq = (
        angular_sq(CX)[: CX // 2 + 1, None, None]
        + angular_sq(N)[None, :, None]
        + angular_sq(N)[None, None, :]
    )
    offset = psq - K0SQ
    denom = (offset * offset + EPS * EPS) * (CX * N * N)
    return np.stack([offset / denom, EPS / denom], axis=1).astype(np.float32)


def halves(value):
    high = value.astype(BF)
    return high, (value - high.astype(F32)).astype(BF)


def from_right(value, table):
    high, low = halves(value)
    out = jnp.dot(high, table[0], preferred_element_type=F32)
    out += jnp.dot(low, table[0], preferred_element_type=F32)
    return out + jnp.dot(high, table[1], preferred_element_type=F32)


def from_left(table, value):
    high, low = halves(value)
    out = jnp.dot(table[0], high, preferred_element_type=F32)
    out += jnp.dot(table[0], low, preferred_element_type=F32)
    return out + jnp.dot(table[1], high, preferred_element_type=F32)


def z_product(planes, table):
    count = planes[0][0].shape[0]
    tall = jnp.concatenate([jnp.concatenate([re, im], axis=1) for re, im in planes], axis=0)
    out = from_right(tall, table)
    parts = [out[k * count : (k + 1) * count] for k in range(len(planes))]
    return [(part[:, :N], part[:, N:]) for part in parts]


def y_product(planes, table):
    wide = jnp.concatenate(
        [jnp.concatenate([plane[part] for plane in planes], axis=1) for part in range(2)], axis=0
    )
    out = from_left(table, wide)
    parts = [out[:, k * N : (k + 1) * N] for k in range(len(planes))]
    return [(part[:N], part[N:]) for part in parts]


def transform(product, table, ref, count, group):
    def one(first):
        planes = [(ref[0, first + k], ref[1, first + k]) for k in range(group)]
        for k, (re, im) in enumerate(product(planes, table)):
            ref[0, first + k] = re
            ref[1, first + k] = im

    if count == group:
        one(0)
    else:
        pl.loop(0, count // group)(lambda i: one(i * group))


def times_root(value, step, length):
    re, im = value
    step %= length
    if step == 0:
        return value
    if 4 * step == length:
        return -im, re
    if 2 * step == length:
        return -re, -im
    if 4 * step == 3 * length:
        return im, -re
    c = math.cos(2.0 * math.pi * step / length)
    s = math.sin(2.0 * math.pi * step / length)
    if 8 * step % length == 0:
        h = math.sqrt(0.5)
        sc, ss = math.copysign(1.0, c), math.copysign(1.0, s)
        first = re - im if sc == ss else re + im
        second = re + im if sc == ss else im - re
        return first * (h * sc), second * (h * sc)
    return re * c - im * s, re * s + im * c


def fft(values, sign):
    count = len(values)
    if count == 1:
        return values
    even = fft(values[0::2], sign)
    odd = fft(values[1::2], sign)
    first, second = [], []
    for k in range(count // 2):
        re, im = times_root(odd[k], sign * k, count)
        first.append((even[k][0] + re, even[k][1] + im))
        second.append((even[k][0] - re, even[k][1] - im))
    return first + second


def fft_of_first(values, count):
    given = len(values)
    ratio = count // given
    out = [None] * count
    for k in range(ratio):
        turned = [times_root(value, -n * k, count) for n, value in enumerate(values)]
        out[k::ratio] = fft(turned, -1)
    return out


def filtered(spectrum, green, rows):
    scaled = []
    for k, (re, im) in enumerate(spectrum):
        g_re = green[min(k, CX - k), 0, rows, :]
        g_im = green[min(k, CX - k), 1, rows, :]
        scaled.append((re * g_re - im * g_im, re * g_im + im * g_re))
    return fft(scaled, 1)


def tiles(count, size):
    def wrap(step):
        pl.loop(0, count // size)(lambda t: step(pl.ds(pl.multiple_of(t * size, size), size)))

    return wrap


def mixed(mix_ref, row, first, source):
    total = mix_ref[row, first] * source[0]
    for r in range(1, len(source)):
        total += mix_ref[row, first + r] * source[r]
    return total


def cut_kernel(place_ref, field_ref, side_ref, first_ref, near_ref, sems):
    far, near, rows = place_ref[0], place_ref[1], pl.multiple_of(place_ref[2], RIM)
    copies = [
        pltpu.make_async_copy(field_ref.at[:, :, pl.ds(rows, RIM), :], side_ref, sems.at[0]),
        pltpu.make_async_copy(field_ref.at[:, pl.ds(far, LEAD)], first_ref, sems.at[1]),
        pltpu.make_async_copy(field_ref.at[:, pl.ds(near, RIM)], near_ref, sems.at[2]),
    ]
    for copy in copies:
        copy.start()
    for copy in copies:
        copy.wait()


def by_depth(coupling_ref, side, b):
    rows = lax.broadcasted_iota(jnp.int32, (RIM, N), 0)
    column = jnp.zeros((RIM, N), F32)
    for a in range(RIM):
        value = coupling_ref[a, RIM - 1 - b] if side == 0 else coupling_ref[RIM - 1 - a, b]
        column = jnp.where(rows == a, value, column)
    return column


def spectrum_kernel(
    place_ref, x_ref, y_coupling_ref, field_ref, forward_ref, inverse_ref, after_ref,
    mix_x_ref, mix_far_ref, mix_y_ref, out_ref, z_ref, y_ref, planes_ref, sem,
):
    far = place_ref[0]
    copy = pltpu.make_async_copy(field_ref.at[:, pl.ds(far + LEAD, REST)], planes_ref, sem)
    copy.start()
    odd = far > 0
    for a in range(RIM):
        for b in range(RIM):
            low, high = x_ref[a, RIM - 1 - b], x_ref[RIM - 1 - a, b]
            mix_x_ref[a, b] = low
            mix_x_ref[RIM + a, b] = high
            mix_far_ref[a, b] = jnp.where(odd, high, low)
    for table_ref, halves_ref in ((forward_ref, z_ref), (inverse_ref, y_ref)):
        halves_ref[0], halves_ref[1] = halves(table_ref[...])
    for side in range(2):
        for b in range(RIM):
            mix_y_ref[side, b] = by_depth(y_coupling_ref, side, b)
    copy.wait()
    planes = [(planes_ref[0, k], planes_ref[1, k]) for k in range(REST)]
    for k, (re, im) in enumerate(y_product(z_product(planes, z_ref), y_ref)):
        out_ref[0, k] = re
        out_ref[1, k] = im


def local_kernel(
    side_ref, place_ref, mix_x_ref, mix_y_ref, field_ref, source_ref, wave_ref, near_ref, z_ref,
    after_ref, out_ref,
):
    base = place_ref[0]

    @pl.loop(0, CX)
    def _(x):
        shifted = wave_ref[x] - K0SQ
        re, im = field_ref[0, x], field_ref[1, x]
        to = lax.rem(x + CX - base, CX)
        out_ref[0, to] = shifted * re + EPS * im + source_ref[0, x]
        out_ref[1, to] = shifted * im - EPS * re + source_ref[1, x]
        for part in range(2):
            first = field_ref[part, x, 0:RIM, :]
            last = field_ref[part, x, N - RIM : N, :]
            add_low = mix_y_ref[0, 0] * last[0:1]
            add_high = mix_y_ref[1, 0] * first[0:1]
            for b in range(1, RIM):
                add_low += mix_y_ref[0, b] * last[b : b + 1]
                add_high += mix_y_ref[1, b] * first[b : b + 1]
            out_ref[part, to, 0:RIM, :] += add_low
            out_ref[part, to, N - RIM : N, :] += add_high

    for side, start, other in ((0, 0, CX - RIM), (1, CX - RIM, 0)):
        weight = side_ref[side]
        to = lax.rem(start + CX - base, CX)

        @tiles(N, 16)
        def _(rows):
            for part in range(2):
                source = [
                    field_ref[part, other + r, rows, :] - weight * near_ref[part, r, rows, :]
                    for r in range(RIM)
                ]
                for p in range(RIM):
                    out_ref[part, to + p, rows, :] += mixed(mix_x_ref, side * RIM + p, 0, source)

    transform(z_product, z_ref, out_ref, CX, 16)


def side_kernel(
    side_ref, place_ref, mix_y_ref, face_ref, hat_ref, z_ref, y_ref, green_ref, out_ref, rows_ref, wide_ref
):
    mix_ref = mix_y_ref.at[place_ref[3]]

    @pl.loop(0, CX)
    def _(x):
        for part in range(2):
            tile = face_ref[part, lax.rem(x + place_ref[0], CX)]
            total = mix_ref[0] * tile[0:1]
            for b in range(1, RIM):
                total += mix_ref[b] * tile[b : b + 1]
            rows_ref[pl.ds(pl.multiple_of(x * RIM, RIM), RIM), part * N : (part + 1) * N] = -total

    wide_ref[...] = from_right(rows_ref[...], z_ref)
    low, high = side_ref[2], side_ref[3]
    group = 16

    def with_side(part, x, term):
        value = hat_ref[part, x]
        return jnp.concatenate(
            [value[:RIM] + low * term, value[RIM : N - RIM], value[N - RIM :] + high * term], axis=0
        )

    @pl.loop(0, CX // group)
    def _(i):
        terms = wide_ref[pl.ds(pl.multiple_of(i * group * RIM, group * RIM), group * RIM), :]
        planes = []
        for k in range(group):
            term = terms[k * RIM : (k + 1) * RIM]
            x = i * group + k
            planes.append((with_side(0, x, term[:, :N]), with_side(1, x, term[:, N:])))
        for k, (re, im) in enumerate(y_product(planes, y_ref)):
            out_ref[0, i * group + k] = re
            out_ref[1, i * group + k] = im

    @tiles(N, 8)
    def _(rows):
        given = [(out_ref[0, x, rows, :], out_ref[1, x, rows, :]) for x in range(CX)]
        for x, (re, im) in enumerate(filtered(fft(given, -1), green_ref, rows)):
            out_ref[0, x, rows, :] = re
            out_ref[1, x, rows, :] = im


def first_kernel(mix_ref, face_ref, z_ref, y_ref, after_ref, out_ref):
    @tiles(N, 16)
    def _(rows):
        for part in range(2):
            source = [face_ref[part, r, rows, :] for r in range(LEAD)]
            for p in range(RIM):
                out_ref[part, p, rows, :] = -mixed(mix_ref, p, 0, source)

    transform(z_product, z_ref, out_ref, RIM, RIM)
    transform(y_product, y_ref, out_ref, RIM, RIM)


def damped(re, im, back, wave):
    ratio = wave * (1.0 / EPS) - K0SQ / EPS
    return back[0] + ratio * (im - back[1]), back[1] - ratio * (re - back[0])


def early_kernel(
    place_ref, mix_ref, second_ref, first_ref, part_ref, line_ref, field_ref, wave_ref, y_ref, z_ref,
    hat_ref, out_ref, work_ref,
):
    base = place_ref[0]

    @tiles(N, 8)
    def _(rows):
        given = []
        for part in range(2):
            source = [second_ref[part, r, rows, :] for r in range(REST)]
            given.append(
                [first_ref[part, p, rows, :] - mixed(mix_ref, p, LEAD, source) for p in range(RIM)]
            )
            for p, value in enumerate(given[part]):
                hat_ref[part, p, rows, :] = value
        lines = [(line_ref[d, 0, rows, :], line_ref[d, 1, rows, :]) for d in range(RIM)]
        for p in range(LEAD):
            re = part_ref[0, p, rows, :]
            im = part_ref[1, p, rows, :]
            for q, (t_re, t_im) in enumerate(zip(*given)):
                g_re, g_im = lines[abs(p - q)]
                re += t_re * g_re - t_im * g_im
                im += t_re * g_im + t_im * g_re
            work_ref[0, p, rows, :] = re
            work_ref[1, p, rows, :] = im

    planes = [(work_ref[0, k], work_ref[1, k]) for k in range(LEAD)]
    for k, back in enumerate(z_product(y_product(planes, y_ref), z_ref)):
        re, im = damped(field_ref[0, base + k], field_ref[1, base + k], back, wave_ref[base + k])
        out_ref[0, k] = re
        out_ref[1, k] = im


def filter_far(given_of, part_ref, green_ref, z_ref, ring_refs, work_ref):
    ring = len(ring_refs)

    @pl.loop(0, N // (8 * ring))
    def _(i):
        for j, ring_ref in enumerate(ring_refs):
            rows = pl.ds(pl.multiple_of(i * 8 * ring, 8 * ring) + 8 * j, 8)
            spectrum = fft_of_first(given_of(rows), CX)
            for x, (re, im) in enumerate(filtered(spectrum, green_ref, rows)):
                ring_ref[0, x] = part_ref[0, x, rows, :] + re
                ring_ref[1, x] = part_ref[1, x, rows, :] + im
            planes = [(ring_ref[0, x], ring_ref[1, x]) for x in range(CX)]
            for x, (re, im) in enumerate(z_product(planes, z_ref)):
                work_ref[0, x, rows, :] = re
                work_ref[1, x, rows, :] = im


def step_back(base, first, group, work_ref, field_ref, wave_ref, y_ref, out_ref):
    planes = [(work_ref[0, first + k], work_ref[1, first + k]) for k in range(group)]
    for k, back in enumerate(y_product(planes, y_ref)):
        x = lax.rem(first + k + base, CX)
        re, im = damped(field_ref[0, x], field_ref[1, x], back, wave_ref[x])
        out_ref[0, x] = re
        out_ref[1, x] = im


def middle_kernel(
    place_ref, hat_ref, part_ref, green_ref, field_ref, wave_ref, yi_ref, zi_ref, z_ref, y_ref,
    out_ref, side_ref, near_ref, second_ref, work_ref, *ring_refs,
):
    base = place_ref[0]

    def given_of(rows):
        return [(hat_ref[0, p, rows, :], hat_ref[1, p, rows, :]) for p in range(RIM)]

    filter_far(given_of, part_ref, green_ref, zi_ref, ring_refs, work_ref)
    for first in (0, 16):
        step_back(base, first, 16, work_ref, field_ref, wave_ref, yi_ref, out_ref)

    cut = pl.ds(pl.multiple_of(place_ref[2], RIM), RIM)
    for part in range(2):
        side_ref[part] = out_ref[part, :, cut, :]
        near_ref[part] = out_ref[part, pl.ds(place_ref[1], RIM)]
    planes = [(out_ref[0, base + k], out_ref[1, base + k]) for k in range(LEAD, RIM)]
    for k, (re, im) in enumerate(y_product(z_product(planes, z_ref), y_ref)):
        second_ref[0, k] = re
        second_ref[1, k] = im


def last_kernel(
    place_ref, mix_ref, second_ref, first_ref, part_ref, green_ref, field_ref, wave_ref, yi_ref, zi_ref,
    out_ref, work_ref, done_ref, sems, *ring_refs,
):
    def given_of(rows):
        sums = []
        for part in range(2):
            source = [second_ref[part, r, rows, :] for r in range(REST)]
            sums.append(
                [first_ref[part, p, rows, :] - mixed(mix_ref, p, LEAD, source) for p in range(RIM)]
            )
        return list(zip(*sums))

    base = place_ref[0]
    filter_far(given_of, part_ref, green_ref, zi_ref, ring_refs, work_ref)
    copies = []
    for first in range(0, CX, RIM):
        step_back(base, first, RIM, work_ref, field_ref, wave_ref, yi_ref, done_ref)
        span = pl.ds(lax.rem(base + first, CX), RIM)
        sem = sems.at[first // RIM]
        copies.append(pltpu.make_async_copy(done_ref.at[:, span], out_ref.at[:, span], sem))
        copies[-1].start()
    for copy in copies:
        copy.wait()


SMEM = pl.BlockSpec(memory_space=pltpu.SMEM)
WHOLE = pl.BlockSpec(memory_space=pltpu.VMEM)


def array(*shape):
    return jax.ShapeDtypeStruct(shape, F32)


VOLUME = array(2, CX, N, N)
FACE = array(2, RIM, N, N)
PART = array(2, LEAD, N, N)
OTHER = array(2, REST, N, N)
SIDE = array(2, CX, RIM, N)
RINGS = (array(2, CX, 8, N),) * RING


PARAMS = pltpu.CompilerParams(vmem_limit_bytes=VMEM_LIMIT)


def cost(weight):
    return pl.CostEstimate(flops=weight * 10**9, bytes_accessed=weight * 10**6, transcendentals=0)


COST = cost(1)


def call(kernel, scalars, operands, out, scratch=(), after=None, weight=1):
    later = [] if after is None else [after]
    return pl.pallas_call(
        kernel,
        in_specs=[SMEM] * len(scalars) + [WHOLE] * len(operands)
        + [pl.BlockSpec(memory_space=pl.ANY)] * len(later),
        out_specs=jax.tree.map(lambda _: WHOLE, out),
        out_shape=out,
        scratch_shapes=[pltpu.VMEM(s.shape, s.dtype) for s in scratch],
        compiler_params=PARAMS,
        cost_estimate=cost(weight),
    )(*scalars, *operands, *later)


HBM = pl.BlockSpec(memory_space=pltpu.HBM)


def prepare(place, coupling_x, coupling_y, field, forward, inverse, after):
    table = jax.ShapeDtypeStruct((2, 2 * N, 2 * N), BF)
    return pl.pallas_call(
        spectrum_kernel,
        in_specs=[SMEM] * 3 + [HBM] + [WHOLE] * 2 + [pl.BlockSpec(memory_space=pl.ANY)],
        out_specs=(SMEM,) * 2 + (WHOLE,) * 4,
        out_shape=(
            array(2 * RIM, RIM), array(RIM, RIM), array(2, RIM, RIM, N), OTHER, table, table
        ),
        scratch_shapes=[pltpu.VMEM(OTHER.shape, F32), pltpu.SemaphoreType.DMA],
        compiler_params=PARAMS,
        cost_estimate=COST,
    )(place, coupling_x, coupling_y, field, forward, inverse, after)


def cut_faces(place, field):
    return pl.pallas_call(
        cut_kernel,
        in_specs=[SMEM, HBM],
        out_specs=(WHOLE,) * 3,
        out_shape=(SIDE, PART, FACE),
        scratch_shapes=[pltpu.SemaphoreType.DMA((3,))],
        compiler_params=PARAMS,
        cost_estimate=COST,
    )(place, field)


def body(field, source, wave, coupling_x, coupling_y):
    n_gx = lax.axis_size("gx")
    n_gy = lax.axis_size("gy")
    gx = lax.axis_index("gx")
    gy = lax.axis_index("gy")
    odd = gx % 2
    near_pairs = [(i, i ^ 1) for i in range(n_gx)]
    far_pairs = [(i, ((i + 1) ^ 1) - 1) for i in range(1, n_gx - 1)]
    side_pairs = [(i, i ^ 1) for i in range(n_gy)]

    forward, inverse = (jnp.asarray(t, F32) for t in dft_tables())
    green = jnp.asarray(green_table())
    lines = jnp.asarray(green_lines())

    weights = jnp.stack([odd, 1 - odd, gy, 1 - gy]).astype(F32)
    span = CX - RIM
    place = jnp.stack([odd * span, (1 - odd) * span, (1 - gy) * (N - RIM), 1 - gy]).astype(jnp.int32)
    pinned = pltpu.with_memory_space_constraint(field, pltpu.HBM)
    side_out, first_out, near_out = cut_faces(place, pinned)
    mix_x, mix_far, mix_y, second_out, zf, zi = prepare(
        place, coupling_x, coupling_y, pinned, forward, inverse, first_out
    )
    yf, yi = zi, zf
    for step in range(2):
        side_in = lax.ppermute(side_out, "gy", side_pairs)
        first_in = lax.ppermute(first_out, "gx", far_pairs)
        near_in = lax.ppermute(near_out, "gx", near_pairs)
        second_in = lax.ppermute(second_out, "gx", far_pairs)
        rows = array(CX * RIM, 2 * N)

        def far_part(after):
            return call(
                first_kernel, (mix_far,), (first_in, zf, yf), FACE, after=after, weight=60
            )

        first = far_part(place) if step == 1 else None
        hat = call(
            local_kernel, (weights, place, mix_x), (mix_y, field, source, wave, near_in, zf), VOLUME,
            after=place if first is None else first,
        )
        part = call(
            side_kernel, (weights, place), (mix_y, side_in, hat, zf, yf, green), VOLUME, (rows, rows),
            weight=30,
        )
        if first is None:
            first = far_part(part)
        if step == 0:
            whole, first_out = call(
                early_kernel, (place, mix_far),
                (second_in, first, part, lines, field, wave, yi, zi), (FACE, PART), (PART,),
            )
            field, side_out, near_out, second_out = call(
                middle_kernel, (place,), (whole, part, green, field, wave, yi, zi, zf, yf),
                (VOLUME, SIDE, FACE, OTHER), (VOLUME, *RINGS),
            )
        else:
            field = pl.pallas_call(
                last_kernel,
                in_specs=[SMEM] * 2 + [WHOLE] * 8,
                out_specs=pl.BlockSpec(memory_space=pltpu.HBM),
                out_shape=VOLUME,
                scratch_shapes=[
                    pltpu.VMEM(VOLUME.shape, F32),
                    pltpu.VMEM(VOLUME.shape, F32),
                    pltpu.SemaphoreType.DMA((CX // RIM,)),
                    *(pltpu.VMEM(r.shape, F32) for r in RINGS),
                ],
                compiler_params=PARAMS,
                cost_estimate=COST,
            )(place, mix_far, second_in, first, part, green, field, wave, yi, zi)
    return field


def solution(mesh):
    placed = (P(None, "gx", "gy", None), P(None, "gx", "gy", None), P("gx", "gy", None), P(), P())
    return jax.shard_map(
        body, mesh=mesh, in_specs=placed, out_specs=P(None, "gx", "gy", None), check_vma=False
    )
```

```python
import functools
import math

import jax
import jax.numpy as jnp
import numpy as np
from jax import lax
from jax.experimental import pallas as pl
from jax.experimental.pallas import tpu as pltpu
from jax.sharding import PartitionSpec as P

RIM = 8
LEAD = 3
REST = RIM - LEAD
RING = 8
K0SQ = 2.4674
EPS = 2.5
CX = 32
N = 128
BF = jnp.bfloat16
F32 = jnp.float32
VMEM_LIMIT = 24 * 1024 * 1024


def dft_tables():
    index = np.arange(N)
    angle = 2.0 * np.pi / N * (index[:, None] * index[None, :] % N)
    cosine, sine = np.cos(angle), np.sin(angle)
    forward = np.block([[cosine, -sine], [sine, cosine]])
    inverse = np.block([[cosine, sine], [-sine, cosine]])
    return forward, inverse


def angular_sq(length):
    freq = 2.0 * np.pi * np.fft.fftfreq(length)
    return freq * freq


def green_lines():
    table = green_table().astype(np.float64)
    both = np.concatenate([table, table[-2:0:-1]])
    lines = CX * np.fft.ifft(both[:, 0] + 1j * both[:, 1], axis=0)[:RIM]
    return np.stack([lines.real, lines.imag], axis=1).astype(np.float32)


def green_table():
    psq = (
        angular_sq(CX)[: CX // 2 + 1, None, None]
        + angular_sq(N)[None, :, None]
        + angular_sq(N)[None, None, :]
    )
    offset = psq - K0SQ
    denom = (offset * offset + EPS * EPS) * (CX * N * N)
    return np.stack([offset / denom, EPS / denom], axis=1).astype(np.float32)


def halves(value):
    high = value.astype(BF)
    return high, (value - high.astype(F32)).astype(BF)


def from_right(value, table):
    high, low = halves(value)
    out = jnp.dot(high, table[0], preferred_element_type=F32)
    out += jnp.dot(low, table[0], preferred_element_type=F32)
    return out + jnp.dot(high, table[1], preferred_element_type=F32)


def from_left(table, value):
    high, low = halves(value)
    out = jnp.dot(table[0], high, preferred_element_type=F32)
    out += jnp.dot(table[0], low, preferred_element_type=F32)
    return out + jnp.dot(table[1], high, preferred_element_type=F32)


def z_product(planes, table):
    count = planes[0][0].shape[0]
    tall = jnp.concatenate([jnp.concatenate([re, im], axis=1) for re, im in planes], axis=0)
    out = from_right(tall, table)
    parts = [out[k * count : (k + 1) * count] for k in range(len(planes))]
    return [(part[:, :N], part[:, N:]) for part in parts]


def y_product(planes, table):
    wide = jnp.concatenate(
        [jnp.concatenate([plane[part] for plane in planes], axis=1) for part in range(2)], axis=0
    )
    out = from_left(table, wide)
    parts = [out[:, k * N : (k + 1) * N] for k in range(len(planes))]
    return [(part[:N], part[N:]) for part in parts]


def transform(product, table, ref, count, group):
    def one(first):
        planes = [(ref[0, first + k], ref[1, first + k]) for k in range(group)]
        for k, (re, im) in enumerate(product(planes, table)):
            ref[0, first + k] = re
            ref[1, first + k] = im

    if count == group:
        one(0)
    else:
        pl.loop(0, count // group)(lambda i: one(i * group))


def times_root(value, step, length):
    re, im = value
    step %= length
    if step == 0:
        return value
    if 4 * step == length:
        return -im, re
    if 2 * step == length:
        return -re, -im
    if 4 * step == 3 * length:
        return im, -re
    c = math.cos(2.0 * math.pi * step / length)
    s = math.sin(2.0 * math.pi * step / length)
    if 8 * step % length == 0:
        h = math.sqrt(0.5)
        sc, ss = math.copysign(1.0, c), math.copysign(1.0, s)
        first = re - im if sc == ss else re + im
        second = re + im if sc == ss else im - re
        return first * (h * sc), second * (h * sc)
    return re * c - im * s, re * s + im * c


def fft(values, sign):
    count = len(values)
    if count == 1:
        return values
    even = fft(values[0::2], sign)
    odd = fft(values[1::2], sign)
    first, second = [], []
    for k in range(count // 2):
        re, im = times_root(odd[k], sign * k, count)
        first.append((even[k][0] + re, even[k][1] + im))
        second.append((even[k][0] - re, even[k][1] - im))
    return first + second


def fft_of_first(values, count):
    given = len(values)
    ratio = count // given
    out = [None] * count
    for k in range(ratio):
        turned = [times_root(value, -n * k, count) for n, value in enumerate(values)]
        out[k::ratio] = fft(turned, -1)
    return out


def filtered(spectrum, green, rows):
    scaled = []
    for k, (re, im) in enumerate(spectrum):
        g_re = green[min(k, CX - k), 0, rows, :]
        g_im = green[min(k, CX - k), 1, rows, :]
        scaled.append((re * g_re - im * g_im, re * g_im + im * g_re))
    return fft(scaled, 1)


def tiles(count, size):
    def wrap(step):
        pl.loop(0, count // size)(lambda t: step(pl.ds(pl.multiple_of(t * size, size), size)))

    return wrap


def mixed(mix_ref, row, first, source):
    total = mix_ref[row, first] * source[0]
    for r in range(1, len(source)):
        total += mix_ref[row, first + r] * source[r]
    return total


def cut_kernel(place_ref, field_ref, side_ref, first_ref, near_ref, sems):
    far, near, rows = place_ref[0], place_ref[1], pl.multiple_of(place_ref[2], RIM)
    copies = [
        pltpu.make_async_copy(field_ref.at[:, :, pl.ds(rows, RIM), :], side_ref, sems.at[0]),
        pltpu.make_async_copy(field_ref.at[:, pl.ds(far, LEAD)], first_ref, sems.at[1]),
        pltpu.make_async_copy(field_ref.at[:, pl.ds(near, RIM)], near_ref, sems.at[2]),
    ]
    for copy in copies:
        copy.start()
    for copy in copies:
        copy.wait()


def by_depth(coupling_ref, side, b):
    rows = lax.broadcasted_iota(jnp.int32, (RIM, N), 0)
    column = jnp.zeros((RIM, N), F32)
    for a in range(RIM):
        value = coupling_ref[a, RIM - 1 - b] if side == 0 else coupling_ref[RIM - 1 - a, b]
        column = jnp.where(rows == a, value, column)
    return column


def spectrum_kernel(
    place_ref, x_ref, y_coupling_ref, field_ref, forward_ref, inverse_ref, after_ref,
    mix_x_ref, mix_far_ref, mix_y_ref, out_ref, z_ref, y_ref, planes_ref, sem,
):
    far = place_ref[0]
    copy = pltpu.make_async_copy(field_ref.at[:, pl.ds(far + LEAD, REST)], planes_ref, sem)
    copy.start()
    odd = far > 0
    for a in range(RIM):
        for b in range(RIM):
            low, high = x_ref[a, RIM - 1 - b], x_ref[RIM - 1 - a, b]
            mix_x_ref[a, b] = low
            mix_x_ref[RIM + a, b] = high
            mix_far_ref[a, b] = jnp.where(odd, high, low)
    for table_ref, halves_ref in ((forward_ref, z_ref), (inverse_ref, y_ref)):
        halves_ref[0], halves_ref[1] = halves(table_ref[...])
    for side in range(2):
        for b in range(RIM):
            mix_y_ref[side, b] = by_depth(y_coupling_ref, side, b)
    copy.wait()
    planes = [(planes_ref[0, k], planes_ref[1, k]) for k in range(REST)]
    for k, (re, im) in enumerate(y_product(z_product(planes, z_ref), y_ref)):
        out_ref[0, k] = re
        out_ref[1, k] = im


def local_kernel(
    side_ref, place_ref, mix_x_ref, mix_y_ref, field_ref, source_ref, wave_ref, near_ref, z_ref,
    after_ref, out_ref,
):
    base = place_ref[0]

    @pl.loop(0, CX)
    def _(x):
        shifted = wave_ref[x] - K0SQ
        re, im = field_ref[0, x], field_ref[1, x]
        to = lax.rem(x + CX - base, CX)
        out_ref[0, to] = shifted * re + EPS * im + source_ref[0, x]
        out_ref[1, to] = shifted * im - EPS * re + source_ref[1, x]
        for part in range(2):
            first = field_ref[part, x, 0:RIM, :]
            last = field_ref[part, x, N - RIM : N, :]
            add_low = mix_y_ref[0, 0] * last[0:1]
            add_high = mix_y_ref[1, 0] * first[0:1]
            for b in range(1, RIM):
                add_low += mix_y_ref[0, b] * last[b : b + 1]
                add_high += mix_y_ref[1, b] * first[b : b + 1]
            out_ref[part, to, 0:RIM, :] += add_low
            out_ref[part, to, N - RIM : N, :] += add_high

    for side, start, other in ((0, 0, CX - RIM), (1, CX - RIM, 0)):
        weight = side_ref[side]
        to = lax.rem(start + CX - base, CX)

        @tiles(N, 16)
        def _(rows):
            for part in range(2):
                source = [
                    field_ref[part, other + r, rows, :] - weight * near_ref[part, r, rows, :]
                    for r in range(RIM)
                ]
                for p in range(RIM):
                    out_ref[part, to + p, rows, :] += mixed(mix_x_ref, side * RIM + p, 0, source)

    transform(z_product, z_ref, out_ref, CX, 16)


def side_kernel(
    side_ref, place_ref, mix_y_ref, face_ref, hat_ref, z_ref, y_ref, green_ref, out_ref, rows_ref, wide_ref
):
    mix_ref = mix_y_ref.at[place_ref[3]]

    @pl.loop(0, CX)
    def _(x):
        for part in range(2):
            tile = face_ref[part, lax.rem(x + place_ref[0], CX)]
            total = mix_ref[0] * tile[0:1]
            for b in range(1, RIM):
                total += mix_ref[b] * tile[b : b + 1]
            rows_ref[pl.ds(pl.multiple_of(x * RIM, RIM), RIM), part * N : (part + 1) * N] = -total

    wide_ref[...] = from_right(rows_ref[...], z_ref)
    low, high = side_ref[2], side_ref[3]
    group = 16

    def with_side(part, x, term):
        value = hat_ref[part, x]
        return jnp.concatenate(
            [value[:RIM] + low * term, value[RIM : N - RIM], value[N - RIM :] + high * term], axis=0
        )

    @pl.loop(0, CX // group)
    def _(i):
        terms = wide_ref[pl.ds(pl.multiple_of(i * group * RIM, group * RIM), group * RIM), :]
        planes = []
        for k in range(group):
            term = terms[k * RIM : (k + 1) * RIM]
            x = i * group + k
            planes.append((with_side(0, x, term[:, :N]), with_side(1, x, term[:, N:])))
        for k, (re, im) in enumerate(y_product(planes, y_ref)):
            out_ref[0, i * group + k] = re
            out_ref[1, i * group + k] = im

    @tiles(N, 8)
    def _(rows):
        given = [(out_ref[0, x, rows, :], out_ref[1, x, rows, :]) for x in range(CX)]
        for x, (re, im) in enumerate(filtered(fft(given, -1), green_ref, rows)):
            out_ref[0, x, rows, :] = re
            out_ref[1, x, rows, :] = im


def lines_kernel(hat_ref, y_ref, out_ref):
    group = 16

    @pl.loop(0, CX // group)
    def _(i):
        planes = [(hat_ref[0, i * group + k], hat_ref[1, i * group + k]) for k in range(group)]
        for k, (re, im) in enumerate(y_product(planes, y_ref)):
            out_ref[0, i * group + k] = re
            out_ref[1, i * group + k] = im

    @tiles(N, 8)
    def _(rows):
        given = [(out_ref[0, x, rows, :], out_ref[1, x, rows, :]) for x in range(CX)]
        for x, (re, im) in enumerate(fft(given, -1)):
            out_ref[0, x, rows, :] = re
            out_ref[1, x, rows, :] = im


def late_side_kernel(
    side_ref, place_ref, mix_y_ref, face_ref, part_ref, z_ref, y_ref, out_ref, rows_ref, wide_ref
):
    mix_ref = mix_y_ref.at[place_ref[3]]

    @pl.loop(0, CX)
    def _(x):
        for part in range(2):
            tile = face_ref[part, lax.rem(x + place_ref[0], CX)]
            total = mix_ref[0] * tile[0:1]
            for b in range(1, RIM):
                total += mix_ref[b] * tile[b : b + 1]
            rows_ref[pl.ds(pl.multiple_of(x * RIM, RIM), RIM), part * N : (part + 1) * N] = -total

    wide_ref[...] = from_right(rows_ref[...], z_ref)
    spans = [slice(x * RIM, (x + 1) * RIM) for x in range(CX)]
    spectrum = fft([(wide_ref[span, :N], wide_ref[span, N:]) for span in spans], -1)
    for span, (re, im) in zip(spans, spectrum):
        wide_ref[span, :N] = re
        wide_ref[span, N:] = im
    low, high = side_ref[2], side_ref[3]
    middle = jnp.zeros((N - 2 * RIM, N), F32)
    group = 16

    @pl.loop(0, CX // group)
    def _(i):
        terms = wide_ref[pl.ds(pl.multiple_of(i * group * RIM, group * RIM), group * RIM), :]
        planes = []
        for k in range(group):
            term = terms[k * RIM : (k + 1) * RIM]
            planes.append(
                tuple(
                    jnp.concatenate([low * value, middle, high * value], axis=0)
                    for value in (term[:, :N], term[:, N:])
                )
            )
        for k, (re, im) in enumerate(y_product(planes, y_ref)):
            out_ref[0, i * group + k] = part_ref[0, i * group + k] + re
            out_ref[1, i * group + k] = part_ref[1, i * group + k] + im


def first_kernel(mix_ref, face_ref, z_ref, y_ref, after_ref, out_ref):
    @tiles(N, 16)
    def _(rows):
        for part in range(2):
            source = [face_ref[part, r, rows, :] for r in range(LEAD)]
            for p in range(RIM):
                out_ref[part, p, rows, :] = -mixed(mix_ref, p, 0, source)

    transform(z_product, z_ref, out_ref, RIM, RIM)
    transform(y_product, y_ref, out_ref, RIM, RIM)


def damped(re, im, back, wave):
    ratio = wave * (1.0 / EPS) - K0SQ / EPS
    return back[0] + ratio * (im - back[1]), back[1] - ratio * (re - back[0])


def early_kernel(
    place_ref, mix_ref, second_ref, first_ref, part_ref, line_ref, field_ref, wave_ref, y_ref, z_ref,
    hat_ref, out_ref, work_ref,
):
    base = place_ref[0]

    @tiles(N, 8)
    def _(rows):
        given = []
        for part in range(2):
            source = [second_ref[part, r, rows, :] for r in range(REST)]
            given.append(
                [first_ref[part, p, rows, :] - mixed(mix_ref, p, LEAD, source) for p in range(RIM)]
            )
            for p, value in enumerate(given[part]):
                hat_ref[part, p, rows, :] = value
        lines = [(line_ref[d, 0, rows, :], line_ref[d, 1, rows, :]) for d in range(RIM)]
        for p in range(LEAD):
            re = part_ref[0, p, rows, :]
            im = part_ref[1, p, rows, :]
            for q, (t_re, t_im) in enumerate(zip(*given)):
                g_re, g_im = lines[abs(p - q)]
                re += t_re * g_re - t_im * g_im
                im += t_re * g_im + t_im * g_re
            work_ref[0, p, rows, :] = re
            work_ref[1, p, rows, :] = im

    planes = [(work_ref[0, k], work_ref[1, k]) for k in range(LEAD)]
    for k, back in enumerate(z_product(y_product(planes, y_ref), z_ref)):
        re, im = damped(field_ref[0, base + k], field_ref[1, base + k], back, wave_ref[base + k])
        out_ref[0, k] = re
        out_ref[1, k] = im


def filter_far(given_of, part_ref, green_ref, z_ref, ring_refs, work_ref, filtered_part=True):
    ring = len(ring_refs)

    @pl.loop(0, N // (8 * ring))
    def _(i):
        for j, ring_ref in enumerate(ring_refs):
            rows = pl.ds(pl.multiple_of(i * 8 * ring, 8 * ring) + 8 * j, 8)
            spectrum = fft_of_first(given_of(rows), CX)
            local = [(part_ref[0, x, rows, :], part_ref[1, x, rows, :]) for x in range(CX)]
            if not filtered_part:
                spectrum = [(a + c, b + d) for (a, b), (c, d) in zip(spectrum, local)]
            for x, (re, im) in enumerate(filtered(spectrum, green_ref, rows)):
                ring_ref[0, x] = local[x][0] + re if filtered_part else re
                ring_ref[1, x] = local[x][1] + im if filtered_part else im
            planes = [(ring_ref[0, x], ring_ref[1, x]) for x in range(CX)]
            for x, (re, im) in enumerate(z_product(planes, z_ref)):
                work_ref[0, x, rows, :] = re
                work_ref[1, x, rows, :] = im


def step_back(base, first, group, work_ref, field_ref, wave_ref, y_ref, out_ref):
    planes = [(work_ref[0, first + k], work_ref[1, first + k]) for k in range(group)]
    for k, back in enumerate(y_product(planes, y_ref)):
        x = lax.rem(first + k + base, CX)
        re, im = damped(field_ref[0, x], field_ref[1, x], back, wave_ref[x])
        out_ref[0, x] = re
        out_ref[1, x] = im


def middle_kernel(
    place_ref, hat_ref, part_ref, green_ref, field_ref, wave_ref, yi_ref, zi_ref, z_ref, y_ref,
    out_ref, side_ref, near_ref, second_ref, work_ref, *ring_refs,
):
    base = place_ref[0]

    def given_of(rows):
        return [(hat_ref[0, p, rows, :], hat_ref[1, p, rows, :]) for p in range(RIM)]

    filter_far(given_of, part_ref, green_ref, zi_ref, ring_refs, work_ref)
    for first in (0, 16):
        step_back(base, first, 16, work_ref, field_ref, wave_ref, yi_ref, out_ref)

    cut = pl.ds(pl.multiple_of(place_ref[2], RIM), RIM)
    for part in range(2):
        side_ref[part] = out_ref[part, :, cut, :]
        near_ref[part] = out_ref[part, pl.ds(place_ref[1], RIM)]
    planes = [(out_ref[0, base + k], out_ref[1, base + k]) for k in range(LEAD, RIM)]
    for k, (re, im) in enumerate(y_product(z_product(planes, z_ref), y_ref)):
        second_ref[0, k] = re
        second_ref[1, k] = im


def last_kernel(
    place_ref, mix_ref, second_ref, first_ref, part_ref, green_ref, field_ref, wave_ref, yi_ref, zi_ref,
    out_ref, work_ref, done_ref, sems, *ring_refs,
):
    def given_of(rows):
        sums = []
        for part in range(2):
            source = [second_ref[part, r, rows, :] for r in range(REST)]
            sums.append(
                [first_ref[part, p, rows, :] - mixed(mix_ref, p, LEAD, source) for p in range(RIM)]
            )
        return list(zip(*sums))

    base = place_ref[0]
    filter_far(given_of, part_ref, green_ref, zi_ref, ring_refs, work_ref, filtered_part=False)
    copies = []
    for first in range(0, CX, RIM):
        step_back(base, first, RIM, work_ref, field_ref, wave_ref, yi_ref, done_ref)
        span = pl.ds(lax.rem(base + first, CX), RIM)
        sem = sems.at[first // RIM]
        copies.append(pltpu.make_async_copy(done_ref.at[:, span], out_ref.at[:, span], sem))
        copies[-1].start()
    for copy in copies:
        copy.wait()


SMEM = pl.BlockSpec(memory_space=pltpu.SMEM)
WHOLE = pl.BlockSpec(memory_space=pltpu.VMEM)


def array(*shape):
    return jax.ShapeDtypeStruct(shape, F32)


VOLUME = array(2, CX, N, N)
FACE = array(2, RIM, N, N)
PART = array(2, LEAD, N, N)
OTHER = array(2, REST, N, N)
SIDE = array(2, CX, RIM, N)
RINGS = (array(2, CX, 8, N),) * RING


PARAMS = pltpu.CompilerParams(vmem_limit_bytes=VMEM_LIMIT)


def cost(weight):
    return pl.CostEstimate(flops=weight * 10**9, bytes_accessed=weight * 10**6, transcendentals=0)


COST = cost(1)


def call(kernel, scalars, operands, out, scratch=(), after=None, weight=1):
    later = [] if after is None else [after]
    return pl.pallas_call(
        kernel,
        in_specs=[SMEM] * len(scalars) + [WHOLE] * len(operands)
        + [pl.BlockSpec(memory_space=pl.ANY)] * len(later),
        out_specs=jax.tree.map(lambda _: WHOLE, out),
        out_shape=out,
        scratch_shapes=[pltpu.VMEM(s.shape, s.dtype) for s in scratch],
        compiler_params=PARAMS,
        cost_estimate=cost(weight),
    )(*scalars, *operands, *later)


HBM = pl.BlockSpec(memory_space=pltpu.HBM)


def prepare(place, coupling_x, coupling_y, field, forward, inverse, after):
    table = jax.ShapeDtypeStruct((2, 2 * N, 2 * N), BF)
    return pl.pallas_call(
        spectrum_kernel,
        in_specs=[SMEM] * 3 + [HBM] + [WHOLE] * 2 + [pl.BlockSpec(memory_space=pl.ANY)],
        out_specs=(SMEM,) * 2 + (WHOLE,) * 4,
        out_shape=(
            array(2 * RIM, RIM), array(RIM, RIM), array(2, RIM, RIM, N), OTHER, table, table
        ),
        scratch_shapes=[pltpu.VMEM(OTHER.shape, F32), pltpu.SemaphoreType.DMA],
        compiler_params=PARAMS,
        cost_estimate=COST,
    )(place, coupling_x, coupling_y, field, forward, inverse, after)


def cut_faces(place, field):
    return pl.pallas_call(
        cut_kernel,
        in_specs=[SMEM, HBM],
        out_specs=(WHOLE,) * 3,
        out_shape=(SIDE, PART, FACE),
        scratch_shapes=[pltpu.SemaphoreType.DMA((3,))],
        compiler_params=PARAMS,
        cost_estimate=COST,
    )(place, field)


def body(field, source, wave, coupling_x, coupling_y):
    n_gx = lax.axis_size("gx")
    n_gy = lax.axis_size("gy")
    gx = lax.axis_index("gx")
    gy = lax.axis_index("gy")
    odd = gx % 2
    near_pairs = [(i, i ^ 1) for i in range(n_gx)]
    far_pairs = [(i, ((i + 1) ^ 1) - 1) for i in range(1, n_gx - 1)]
    side_pairs = [(i, i ^ 1) for i in range(n_gy)]

    forward, inverse = (jnp.asarray(t, F32) for t in dft_tables())
    green = jnp.asarray(green_table())
    lines = jnp.asarray(green_lines())

    weights = jnp.stack([odd, 1 - odd, gy, 1 - gy]).astype(F32)
    span = CX - RIM
    place = jnp.stack([odd * span, (1 - odd) * span, (1 - gy) * (N - RIM), 1 - gy]).astype(jnp.int32)
    pinned = pltpu.with_memory_space_constraint(field, pltpu.HBM)
    side_out, first_out, near_out = cut_faces(place, pinned)
    mix_x, mix_far, mix_y, second_out, zf, zi = prepare(
        place, coupling_x, coupling_y, pinned, forward, inverse, first_out
    )
    yf, yi = zi, zf
    for step in range(2):
        side_in = lax.ppermute(side_out, "gy", side_pairs)
        first_in = lax.ppermute(first_out, "gx", far_pairs)
        near_in = lax.ppermute(near_out, "gx", near_pairs)
        second_in = lax.ppermute(second_out, "gx", far_pairs)
        rows = array(CX * RIM, 2 * N)

        def far_part(after):
            return call(
                first_kernel, (mix_far,), (first_in, zf, yf), FACE, after=after, weight=60
            )

        first = far_part(place) if step == 1 else None
        hat = call(
            local_kernel, (weights, place, mix_x), (mix_y, field, source, wave, near_in, zf), VOLUME,
            after=place if first is None else first,
        )
        if step == 0:
            part = call(
                side_kernel, (weights, place), (mix_y, side_in, hat, zf, yf, green), VOLUME, (rows, rows),
                weight=30,
            )
        else:
            lines_in = call(lines_kernel, (), (hat, yf), VOLUME)
            part = call(
                late_side_kernel, (weights, place), (mix_y, side_in, lines_in, zf, yf), VOLUME, (rows, rows),
                weight=30,
            )
        if first is None:
            first = far_part(part)
        if step == 0:
            whole, first_out = call(
                early_kernel, (place, mix_far),
                (second_in, first, part, lines, field, wave, yi, zi), (FACE, PART), (PART,),
            )
            field, side_out, near_out, second_out = call(
                middle_kernel, (place,), (whole, part, green, field, wave, yi, zi, zf, yf),
                (VOLUME, SIDE, FACE, OTHER), (VOLUME, *RINGS),
            )
        else:
            field = pl.pallas_call(
                last_kernel,
                in_specs=[SMEM] * 2 + [WHOLE] * 8,
                out_specs=pl.BlockSpec(memory_space=pltpu.HBM),
                out_shape=VOLUME,
                scratch_shapes=[
                    pltpu.VMEM(VOLUME.shape, F32),
                    pltpu.VMEM(VOLUME.shape, F32),
                    pltpu.SemaphoreType.DMA((CX // RIM,)),
                    *(pltpu.VMEM(r.shape, F32) for r in RINGS),
                ],
                compiler_params=PARAMS,
                cost_estimate=COST,
            )(place, mix_far, second_in, first, part, green, field, wave, yi, zi)
    return field


def solution(mesh):
    placed = (P(None, "gx", "gy", None), P(None, "gx", "gy", None), P("gx", "gy", None), P(), P())
    return jax.shard_map(
        body, mesh=mesh, in_specs=placed, out_specs=P(None, "gx", "gy", None), check_vma=False
    )
```
